128 devices in a mesh: view: 4 (over y), space: 32 (over x, z, core).
Axes of the slice: x: 4, y: 4, z: 4, core: 2. Of those that a mesh axis runs over, the one named last changes fastest.
Arguments:
- estimate: float32 [3072, 128, 128], P('space'), may hold values from 0.5 to 2
- view_data: float32 [4, 3072, 128, 128], P('view', 'space'), may hold values from 0.2 to 5
- blend_weights: float32 [4, 3072, 128, 128], P('view', 'space'), may hold values from 0.1 to 1
- kernels: float32 [4, 3, 31], P('view'), may hold values from 0.01 to 1.1
- shifts: int32 [4], P('view'), may hold values from 0 to 15, as said below
Outputs:
- updated: float32 [3072, 128, 128], P('space')
The draws below stay inside these ranges and needn't reach their ends.
Inputs may be any that keep to these rules, and one draw needn't show every extreme that they name: `shifts`: some view's shift is exactly 15.
All inputs are finite; a program needn't handle non-finite values.
Results may differ from the reference program's by a relative error of at most 0.0001.
Values sent between devices are 32-bit elements; how exact they have to be, the bound alone decides.
No kernel may reach another device: no remote copies, remote signals or barrier semaphores. Data moves between devices by JAX's collectives and lax.ppermute only.
A program may use at most 128 MiB of HBM per device.

```python
import math
import jax
import jax.numpy as jnp
from jax import lax

NY = 128
NX = 128
TAPS = 31
OFF = 16
ITERS = 2
VIEWS = 4
NZ = 3072


def draw_kernels(key, part):
    key = jax.random.fold_in(key, 11)
    width_key, noise_key = jax.random.split(key)
    half_taps = (TAPS - 1) // 2
    offsets = (jnp.arange(TAPS) - half_taps).astype(jnp.float32)
    fraction = jax.random.uniform(width_key, (VIEWS, 3), jnp.float32)
    axial = jnp.exp(jnp.log(2.5) + fraction * (jnp.log(5.0) - jnp.log(2.5)))
    lateral = jnp.exp(jnp.log(1.2) + fraction * (jnp.log(3.0) - jnp.log(1.2)))
    factor_index = jnp.arange(3)[None, :]
    sigma = jnp.where(factor_index == 0, axial, lateral)
    profile = jnp.exp(-offsets[None, None, :] ** 2 / (2.0 * sigma[:, :, None] ** 2))
    noise = jax.random.uniform(noise_key, (VIEWS, 3, TAPS), jnp.float32, 0.9, 1.1)
    values = jnp.maximum(profile * noise, 0.01)
    return values.astype(jnp.float32)


def draw_shifts(key, part):
    key = jax.random.fold_in(key, 7)
    first_key, second_key = jax.random.split(key)
    values = jax.random.randint(first_key, (VIEWS,), 0, OFF)
    chosen = jax.random.randint(second_key, (), 0, VIEWS)
    values = jnp.where(jnp.arange(VIEWS) == chosen, OFF - 1, values)
    return values.astype(jnp.int32)


def level_of(own_key, extent, cuts, low, high):
    loudness = 1.0
    for axis_at, shards_of in cuts:
        heights = jax.random.uniform(jax.random.fold_in(jax.random.fold_in(own_key, 6), axis_at), (shards_of,), jnp.float32, low / len(cuts), high / len(cuts))
        loudness = loudness * jnp.repeat(jnp.exp(heights), extent[axis_at] // shards_of).reshape((-1,) + (1,) * (len(extent) - 1 - axis_at))
    return loudness


def setup_inputs(seed: int = 0) -> dict:
    splits = jax.random.split(jax.random.key(seed), 6)
    estimate = jnp.clip(jnp.exp(math.log(2.0) - 1.3862944 * jax.random.uniform(splits[0], (NZ, NY, NX), jnp.float32) ** level_of(splits[0], (NZ, NY, NX), ((0, 32),), -0.2, 0.2)), 0.5, 2.0)
    view_data = jnp.clip(jnp.exp(math.log(5.0) - 3.218876 * jax.random.uniform(splits[1], (VIEWS, NZ, NY, NX), jnp.float32) ** level_of(splits[1], (VIEWS, NZ, NY, NX), ((0, 4), (1, 32)), -0.2, 0.2)), 0.2, 5.0)
    blend_weights = jnp.clip(0.1 + 0.9 * jax.random.uniform(splits[2], (VIEWS, NZ, NY, NX), jnp.float32) ** level_of(splits[2], (VIEWS, NZ, NY, NX), ((0, 4), (1, 32)), -0.2, 0.2), 0.1, 1.0)
    kernels = draw_kernels(jax.random.fold_in(splits[5], 71), 0)
    shifts = draw_shifts(jax.random.fold_in(splits[5], 71), 0)
    return {"estimate": estimate, "view_data": view_data, "blend_weights": blend_weights, "kernels": kernels, "shifts": shifts}


background_level = 0.1


def band_matrix(kernel, row_count, col_count, lowest, flipped):
    tap_count = kernel.shape[0]
    offset_grid = jnp.arange(col_count)[None, :] - jnp.arange(row_count)[:, None] - lowest
    tap_index = offset_grid if flipped else (tap_count - 1) - offset_grid
    matches = (tap_index[:, :, None] == jnp.arange(tap_count)[None, None, :]).astype(kernel.dtype)
    return jnp.sum(matches * kernel[None, None, :], axis=-1)


def transverse(volume, kernel_y, kernel_x, flipped):
    half_taps = (kernel_y.shape[0] - 1) // 2
    across_y = band_matrix(kernel_y, volume.shape[1], volume.shape[1], -half_taps, flipped)
    across_x = band_matrix(kernel_x, volume.shape[2], volume.shape[2], -half_taps, flipped)
    volume = jnp.einsum('ab,zbx->zax', across_y, volume, precision=lax.Precision.HIGHEST)
    return jnp.einsum('zyb,ab->zya', volume, across_x, precision=lax.Precision.HIGHEST)


def view_correction(estimate, data_one, kernel_set, shift):
    normalized = kernel_set / jnp.sum(kernel_set, axis=1, keepdims=True)
    tap_count = kernel_set.shape[1]
    half_taps = (tap_count - 1) // 2
    span = 2 * half_taps
    depth = estimate.shape[0]
    margin = OFF + 2 * span
    padded = jnp.pad(estimate, ((margin, margin), (0, 0), (0, 0)))
    anchor = (shift + (margin - span)).astype(jnp.int32)
    window = lax.dynamic_slice_in_dim(padded, anchor, depth + 2 * span, 0)
    blurred_z = jnp.zeros_like(window[:depth + span])
    for tap in range(tap_count):
        blurred_z = blurred_z + normalized[0, tap] * window[span - tap:span - tap + depth + span]
    blurred = transverse(blurred_z, normalized[1], normalized[2], False) + background_level
    data_padded = jnp.pad(data_one, ((half_taps, half_taps), (0, 0), (0, 0)))
    quotient = data_padded / blurred
    returned_z = jnp.zeros_like(quotient[:depth])
    for tap in range(tap_count):
        returned_z = returned_z + normalized[0, tap] * quotient[tap:tap + depth]
    returned = transverse(returned_z, normalized[1], normalized[2], True)
    spread = jnp.pad(returned, ((OFF, OFF), (0, 0), (0, 0)))
    return lax.dynamic_slice_in_dim(spread, (OFF - shift).astype(jnp.int32), depth, 0)


def reference(estimate, view_data, blend_weights, kernels, shifts):
    weight_sum = jnp.sum(blend_weights, axis=0)
    for iteration in range(ITERS):
        combined = jnp.zeros_like(estimate)
        for view_index in range(VIEWS):
            correction = view_correction(estimate, view_data[view_index], kernels[view_index], shifts[view_index])
            combined = combined + blend_weights[view_index] * correction
        estimate = estimate * combined / weight_sum
    return estimate
```

```python
import functools

import jax
import jax.numpy as jnp
from jax import lax
from jax.experimental import pallas as pl
from jax.experimental.pallas import tpu as pltpu
from jax.sharding import PartitionSpec as P

F32, BF16 = jnp.float32, jnp.bfloat16
ITERS = 2
BACKGROUND = 0.1
BLOCK = 96
PLANE = 128
RIM = 32
VMEM = 50 << 20
EDGE, INNER = 16, 8
OPPOSITE, PLUS, MINUS, OWN = range(4)
STEP = (2, 1, 3, 0)


def halves(m):
    high = lax.reduce_precision(m, 8, 7)
    return high.astype(BF16), (m - high).astype(BF16)


def split(value):
    high = value.astype(BF16)
    return high, (value - high.astype(F32)).astype(BF16)


def band(taps, rows, cols, index):
    tap = index(jnp.arange(rows)[:, None], jnp.arange(cols)[None, :])
    return jnp.sum(jnp.where(tap[:, :, None] == jnp.arange(taps.shape[0]), taps, 0.0), -1)


def left(m):
    high, low = halves(m)
    return jnp.block([[high, high], [low, jnp.zeros_like(low)]])


def right(m):
    high, low = halves(m)
    return jnp.block([[high, low], [high, jnp.zeros_like(low)]])


def operators(kernels):
    k = kernels / jnp.sum(kernels, axis=1, keepdims=True)
    along_y = band(k[1], PLANE, PLANE, lambda a, b: a - b + 15)
    along_x = band(k[2], PLANE, PLANE, lambda a, b: a - b + 15)
    blur_z = band(k[0], 64, 96, lambda row, col: 31 - (col - row))
    return_z = band(k[0], BLOCK, 128, lambda row, col: col - row - 1)
    return (
        left(along_y), right(along_x.T), left(along_y.T), right(along_x),
        left(blur_z), left(return_z),
    )


def cost(flops, nbytes):
    return pl.CostEstimate(flops=int(flops), bytes_accessed=int(nbytes), transcendentals=0)


PARAMS = pltpu.CompilerParams(vmem_limit_bytes=VMEM)
SQUARE = pl.BlockSpec((256, 256), lambda *_: (0, 0))


def two_planes(first, second, along_y, along_x):
    h0, l0 = split(first)
    h1, l1 = split(second)
    planes = jnp.concatenate(
        [jnp.concatenate([h0, h1], 1), jnp.concatenate([l0, l1], 1)], 0
    )
    out = jnp.dot(along_y, planes, preferred_element_type=F32)
    high, low = split(out[:PLANE] + out[PLANE:])
    rows = jnp.concatenate(
        [
            jnp.concatenate([high[:, :PLANE], low[:, :PLANE]], 1),
            jnp.concatenate([high[:, PLANE:], low[:, PLANE:]], 1),
        ],
        0,
    )
    out = jnp.dot(rows, along_x, preferred_element_type=F32)
    out = out[:, :PLANE] + out[:, PLANE:]
    return out[:PLANE], out[PLANE:]


def lateral_body(in_ref, y_ref, x_ref, out_ref):
    along_y, along_x = y_ref[...], x_ref[...]
    for i in range(0, in_ref.shape[0], 2):
        out_ref[i], out_ref[i + 1] = two_planes(in_ref[i], in_ref[i + 1], along_y, along_x)


def lateral(volume, along_y, along_x, group=16):
    count = volume.shape[0]
    block = pl.BlockSpec((group, PLANE, PLANE), lambda i: (i, 0, 0))
    return pl.pallas_call(
        lateral_body,
        grid=(count // group,),
        in_specs=[block, SQUARE, SQUARE],
        out_specs=block,
        out_shape=jax.ShapeDtypeStruct(volume.shape, F32),
        name="blur_lateral",
        cost_estimate=cost(count / 2 * 2**27, count * 2**17),
        compiler_params=PARAMS,
    )(volume, along_y, along_x)


def place_edge(chunk):
    return 16 * chunk + jnp.where(chunk >= 2, 32, 0)


def pieces_body(place, rows, total, sc_ref, *refs):
    count = len(place)
    pieces, (y_ref, x_ref, out_hbm), (held, out, sem, out_sem) = (
        refs[: 2 * count], refs[2 * count : 2 * count + 3], refs[2 * count + 3 :],
    )
    view = sc_ref[0]
    copies = []
    for i in range(count):
        for half in range(2):
            copies.append(
                pltpu.make_async_copy(
                    pieces[2 * i + half],
                    held.at[pl.ds(i * rows, rows), pl.ds(64 * half, 64)],
                    sem.at[2 * i + half],
                )
            )
            copies[-1].start()
    along_y, along_x = y_ref[...], x_ref[...]
    outs = []
    for i in range(count):
        copies[2 * i].wait()
        copies[2 * i + 1].wait()

        @pl.loop(0, rows // 4)
        def _(j):
            for k in (0, 2):
                row = i * rows + 4 * j + k
                out[row], out[row + 1] = two_planes(held[row], held[row + 1], along_y, along_x)

        outs.append(
            pltpu.make_async_copy(
                out.at[pl.ds(i * rows, rows)],
                out_hbm.at[pl.ds(place[i](view), rows)],
                out_sem.at[i],
            )
        )
        outs[-1].start()
    for copy in outs:
        copy.wait()


def lateral_pieces(scalars, pieces, place, rows, along_y, along_x):
    count = len(pieces)
    total = count * rows
    anywhere = pl.BlockSpec(memory_space=pl.ANY)
    whole = pl.BlockSpec(memory_space=pltpu.VMEM)
    return pl.pallas_call(
        functools.partial(pieces_body, place, rows, total),
        in_specs=[pl.BlockSpec(memory_space=pltpu.SMEM)] + [anywhere] * (2 * count) + [whole] * 2,
        out_specs=anywhere,
        out_shape=jax.ShapeDtypeStruct((total, PLANE, PLANE), F32),
        scratch_shapes=[
            pltpu.VMEM((total, PLANE, PLANE), F32),
            pltpu.VMEM((total, PLANE, PLANE), F32),
            pltpu.SemaphoreType.DMA((2 * count,)),
            pltpu.SemaphoreType.DMA((count,)),
        ],
        name="blur_pieces",
        cost_estimate=cost(total / 2 * 2**27, total * 2**17),
        compiler_params=PARAMS,
    )(scalars, *[half for piece in pieces for half in piece], along_y, along_x)


def axial_body(segments, depth, sc_ref, *refs):
    count = len(segments)
    d_ref, blur_ref, back_ref, out_ref = refs[count:]
    blur_z, return_z = blur_ref[...], back_ref[...]
    start = sc_ref[2]
    for y in range(0, depth, 2):
        high, low = {}, {}
        for ref, places in zip(refs[:count], segments):
            for segment, row in places.items():
                rows = slice(row, row + 32)
                high[segment], low[segment] = split(
                    jnp.concatenate([ref[rows, y, :], ref[rows, y + 1, :]], 1)
                )
        blurred = []
        for first in (0, 2):
            window = jnp.concatenate(
                [high[first + i] for i in range(3)] + [low[first + i] for i in range(3)], 0
            )
            out = jnp.dot(blur_z, window, preferred_element_type=F32)
            blurred.append(out[:64] + out[64:])
        blurred = jnp.concatenate(blurred, 0) + BACKGROUND
        data = jnp.concatenate(
            [d_ref[pl.ds(start, 128), y, :], d_ref[pl.ds(start, 128), y + 1, :]], 1
        )
        quotient = jnp.concatenate(split(data / blurred), 0)
        out = jnp.dot(return_z, quotient, preferred_element_type=F32)
        out = out[:BLOCK] + out[BLOCK:]
        out_ref[:, y, :] = out[:, :PLANE]
        out_ref[:, y + 1, :] = out[:, PLANE:]


def axial(scalars, parts, segments, data, blur_z, return_z, depth=8):
    spec = lambda rows: pl.BlockSpec((rows, depth, PLANE), lambda i, sc: (0, i, 0))
    fixed = lambda m: pl.BlockSpec(m.shape, lambda i, sc: (0, 0))
    return pl.pallas_call(
        functools.partial(axial_body, segments, depth),
        grid_spec=pltpu.PrefetchScalarGridSpec(
            num_scalar_prefetch=1,
            grid=(PLANE // depth,),
            in_specs=[spec(part.shape[0]) for part in parts]
            + [spec(data.shape[0]), fixed(blur_z), fixed(return_z)],
            out_specs=spec(BLOCK),
        ),
        out_shape=jax.ShapeDtypeStruct((BLOCK, PLANE, PLANE), F32),
        name="quotient_axial",
        cost_estimate=cost(64 * 2**27, 400 * 2**16),
        compiler_params=PARAMS,
    )(scalars, *parts, data, blur_z, return_z)


def weighted_body(rows, place, sc_ref, r_ref, w_ref, y_ref, x_ref, *outs):
    step = pl.program_id(0)
    along_y, along_x = y_ref[...], x_ref[...]
    chunk = lax.rem(sc_ref[0] + chunk_step(step), 4)
    first = place(chunk)
    for which in range(4):

        @pl.when(step == which)
        def _():
            for i in range(0, rows, 2):
                pair = two_planes(r_ref[i], r_ref[i + 1], along_y, along_x)
                for k in range(2):
                    value = pair[k] * w_ref[i + k]
                    value = jnp.where(first + i + k >= sc_ref[1], value, 0.0)
                    outs[2 * which][i + k] = value[:64]
                    outs[2 * which + 1][i + k] = value[64:]


def chunk_step(step):
    return jnp.where(step == 0, 2, jnp.where(step == 1, 1, jnp.where(step == 2, 3, 0)))


def weighted(scalars, returned, weights, along_y, along_x, rows, place):
    block = pl.BlockSpec(
        (rows, PLANE, PLANE),
        lambda i, sc: (place(lax.rem(sc[0] + chunk_step(i), 4)) // rows, 0, 0),
    )
    piece = pl.BlockSpec((rows, 64, PLANE), lambda i, sc: (0, 0, 0))
    return pl.pallas_call(
        functools.partial(weighted_body, rows, place),
        grid_spec=pltpu.PrefetchScalarGridSpec(
            num_scalar_prefetch=1,
            grid=(4,),
            in_specs=[block, block, SQUARE, SQUARE],
            out_specs=[piece] * 8,
        ),
        out_shape=[jax.ShapeDtypeStruct((rows, 64, PLANE), F32)] * 8,
        name="return_lateral",
        cost_estimate=cost(2 * rows * 2**27, 12 * rows * 2**16),
        compiler_params=PARAMS,
    )(scalars, returned, weights, along_y, along_x)


def place_inner(chunk):
    return 32 + INNER * chunk


def pick_body(steps, sc_ref, w_ref, *refs):
    outs, sem = refs[:-1], refs[-1]
    copies = []
    for i, step in enumerate(steps):
        chunk = lax.rem(sc_ref[0] + step, 4)
        for half in range(2):
            side = pl.ds(64 * half, 64)
            for k, (row, rows, at) in enumerate(
                ((place_edge(chunk), EDGE, 0), (place_inner(chunk), INNER, EDGE))
            ):
                copies.append(
                    pltpu.make_async_copy(
                        w_ref.at[pl.ds(row, rows), side],
                        outs[2 * i + half].at[pl.ds(at, rows)],
                        sem.at[4 * i + 2 * half + k],
                    )
                )
                copies[-1].start()
    for copy in copies:
        copy.wait()


def pick(scalars, volume, steps):
    anywhere = pl.BlockSpec(memory_space=pl.ANY)
    return pl.pallas_call(
        functools.partial(pick_body, steps),
        in_specs=[pl.BlockSpec(memory_space=pltpu.SMEM), anywhere],
        out_specs=[anywhere] * (2 * len(steps)),
        out_shape=[jax.ShapeDtypeStruct((EDGE + INNER, 64, PLANE), F32)] * (2 * len(steps)),
        scratch_shapes=[pltpu.SemaphoreType.DMA((4 * len(steps),))],
        name="pick_chunks",
        cost_estimate=cost(0, len(steps) * 24 * 2**17),
        compiler_params=PARAMS,
    )(scalars, volume)


def assemble_body(sc_ref, *refs):
    pieces, out, sem = refs[:-2], refs[-2], refs[-1]
    copies = []
    for i in range(8):
        chunk = lax.rem(sc_ref[0] + STEP[i % 4], 4)
        row, rows = (place_edge(chunk), EDGE) if i < 4 else (place_inner(chunk), INNER)
        for half in range(2):
            copies.append(
                pltpu.make_async_copy(
                    pieces[2 * i + half],
                    out.at[pl.ds(row, rows), pl.ds(64 * half, 64)],
                    sem.at[2 * i + half],
                )
            )
            copies[-1].start()
    for copy in copies:
        copy.wait()


def assemble(scalars, edge, inner):
    anywhere = pl.BlockSpec(memory_space=pl.ANY)
    pieces = [half for piece in edge + inner for half in piece]
    return pl.pallas_call(
        assemble_body,
        in_specs=[pl.BlockSpec(memory_space=pltpu.SMEM)] + [anywhere] * 16,
        out_specs=anywhere,
        out_shape=jax.ShapeDtypeStruct((BLOCK, PLANE, PLANE), F32),
        scratch_shapes=[pltpu.SemaphoreType.DMA((16,))],
        name="assemble",
        cost_estimate=cost(0, 96 * 2**17),
        compiler_params=PARAMS,
    )(scalars, *pieces)


def to_plus(value):
    return lax.ppermute(value, "view", [(i, (i + 1) % 4) for i in range(4)])


def to_minus(value):
    return lax.ppermute(value, "view", [(i, (i - 1) % 4) for i in range(4)])


def to_space(value, steps):
    count = lax.axis_size("space")
    pairs = [(i, i + steps) for i in range(count) if 0 <= i + steps < count]
    return lax.ppermute(value, "space", pairs)


def to_rim(value, step):
    count = lax.axis_size("space")
    pairs = []
    for view in range(4):
        move = 1 if (view + step) % 4 >= 2 else -1
        for i in range(count):
            if 0 <= i + move < count:
                pairs.append((view * count + i, view * count + i + move))
    return lax.ppermute(value, ("view", "space"), pairs)


def ring_sum(pieces):
    far_a = to_plus(pieces[0])
    far_b = to_minus(pieces[1])
    left_b = to_plus(pieces[3])
    right_a = to_minus(pieces[4])
    left_a = to_plus(pieces[2] + far_a)
    right_b = to_minus(pieces[5] + far_b)
    return pieces[6] + left_a + right_a, pieces[7] + left_b + right_b


def ring_gather(own):
    own_a, own_b = own
    left_a, right_b = to_plus(own_a), to_minus(own_b)
    left_b, right_a = to_plus(own_b), to_minus(own_a)
    far_a, far_b = to_plus(left_a), to_minus(right_b)
    return [(far_a, far_b), (right_a, right_b), (left_a, left_b), (own_a, own_b)]


def on_device(estimate, view_data, blend_weights, kernels, shifts):
    view, place = lax.axis_index("view"), lax.axis_index("space")
    shift = shifts[0]
    scalars = jnp.stack([view, jnp.where(place == 0, shift, 0), 16 - shift]).astype(jnp.int32)
    data, weights = view_data[0], blend_weights[0]
    blur_y, blur_x, back_y, back_x, blur_z, back_z = operators(kernels[0])

    low = to_space(estimate[BLOCK - RIM :], 1)
    high = to_space(estimate[:RIM], -1)
    data_low = to_space(data[BLOCK - RIM :], 1)
    data_high = to_space(data[:16], -1)

    weight_sum = ring_sum(pick(scalars, weights, STEP))
    own = pick(scalars, estimate, (0,))

    parts = [lateral(part, blur_y, blur_x) for part in (low, estimate, high)]
    segments = [{0: 0}, {1: 0, 2: 32, 3: 64}, {4: 0}]
    data = jnp.concatenate([data_low, data, data_high], 0)

    for iteration in range(ITERS):
        returned = axial(scalars, parts, segments, data, blur_z, back_z)
        edge = weighted(scalars, returned, weights, back_y, back_x, EDGE, place_edge)
        inner = weighted(scalars, returned, weights, back_y, back_x, INNER, place_inner)
        edge, inner = ring_sum(edge), ring_sum(inner)
        own_edge = [e[:EDGE] * c / w[:EDGE] for e, c, w in zip(own, edge, weight_sum)]
        own_inner = [e[EDGE:] * c / w[EDGE:] for e, c, w in zip(own, inner, weight_sum)]
        own = [jnp.concatenate([e, i], 0) for e, i in zip(own_edge, own_inner)]
        edge, inner = ring_gather(own_edge), ring_gather(own_inner)
        if iteration == ITERS - 1:
            return assemble(scalars, edge, inner)
        rim = [tuple(to_rim(half, step) for half in piece) for piece, step in zip(edge, STEP)]

        def inside(step):
            return lambda v: 32 + EDGE * lax.rem(v + step, 4)

        def beyond(step):
            def at(v):
                chunk = lax.rem(v + step, 4)
                return jnp.where(chunk >= 2, EDGE * (chunk - 2), 96 + EDGE * chunk)
            return at

        def middle(step):
            return lambda v: INNER * lax.rem(v + step, 4)

        parts = [
            lateral_pieces(
                scalars, edge + rim, [inside(s) for s in STEP] + [beyond(s) for s in STEP],
                EDGE, blur_y, blur_x,
            ),
            lateral_pieces(scalars, inner, [middle(s) for s in STEP], INNER, blur_y, blur_x),
        ]
        segments = [{0: 0, 1: 32, 3: 64, 4: 96}, {2: 0}]


def solution(mesh):
    return jax.shard_map(
        on_device,
        mesh=mesh,
        in_specs=(
            P("space", None, None),
            P("view", "space", None, None),
            P("view", "space", None, None),
            P("view", None, None),
            P("view"),
        ),
        out_specs=P("space", None, None),
        check_vma=False,
    )
```

```python
import functools

import jax
import jax.numpy as jnp
from jax import lax
from jax.experimental import pallas as pl
from jax.experimental.pallas import tpu as pltpu
from jax.sharding import PartitionSpec as P

F32, BF16 = jnp.float32, jnp.bfloat16
ITERS = 2
BACKGROUND = 0.1
BLOCK = 96
BATCH = 32
CHUNK = 8
PLANE = 128
VMEM = 50 << 20
STEP = (2, 1, 3, 0)


def halves(m):
    high = lax.reduce_precision(m, 8, 7)
    return high.astype(BF16), (m - high).astype(BF16)


def split(value):
    high = value.astype(BF16)
    return high, (value - high.astype(F32)).astype(BF16)


def band(taps, rows, cols, index):
    tap = index(jnp.arange(rows)[:, None], jnp.arange(cols)[None, :])
    return jnp.sum(jnp.where(tap[:, :, None] == jnp.arange(taps.shape[0]), taps, 0.0), -1)


def left(m):
    high, low = halves(m)
    return jnp.block([[high, high], [low, jnp.zeros_like(low)]])


def right(m):
    high, low = halves(m)
    return jnp.block([[high, low], [high, jnp.zeros_like(low)]])


def operators(kernels):
    k = kernels / jnp.sum(kernels, axis=1, keepdims=True)
    along_y = band(k[1], PLANE, PLANE, lambda a, b: a - b + 15)
    along_x = band(k[2], PLANE, PLANE, lambda a, b: a - b + 15)
    blur_z = band(k[0], 2 * BATCH, 3 * BATCH, lambda row, col: 31 - (col - row))
    return_z = band(k[0], BATCH, 2 * BATCH, lambda row, col: col - row - 1)
    return (
        left(along_y), right(along_x.T), left(along_y.T), right(along_x),
        left(blur_z), left(return_z),
    )


def cost(us):
    return pl.CostEstimate(flops=int(us * 1.15e9), bytes_accessed=0, transcendentals=0)


PARAMS = pltpu.CompilerParams(vmem_limit_bytes=VMEM)
ANYWHERE = pl.BlockSpec(memory_space=pl.ANY)
WHOLE = pl.BlockSpec(memory_space=pltpu.VMEM)
SCALARS = pl.BlockSpec(memory_space=pltpu.SMEM)
SEGMENT = jax.ShapeDtypeStruct((PLANE, BATCH, PLANE), F32)
PIECE = jax.ShapeDtypeStruct((CHUNK, PLANE // 2, PLANE), F32)


def two_planes(first, second, along_y, along_x):
    h0, l0 = split(first)
    h1, l1 = split(second)
    planes = jnp.concatenate(
        [jnp.concatenate([h0, h1], 1), jnp.concatenate([l0, l1], 1)], 0
    )
    out = jnp.dot(along_y, planes, preferred_element_type=F32)
    high, low = split(out[:PLANE] + out[PLANE:])
    rows = jnp.concatenate(
        [
            jnp.concatenate([high[:, :PLANE], low[:, :PLANE]], 1),
            jnp.concatenate([high[:, PLANE:], low[:, PLANE:]], 1),
        ],
        0,
    )
    out = jnp.dot(rows, along_x, preferred_element_type=F32)
    out = out[:, :PLANE] + out[:, PLANE:]
    return out[:PLANE], out[PLANE:]


def own_body(in_ref, y_ref, x_ref, *outs):
    step = pl.program_id(0)
    along_y, along_x = y_ref[...], x_ref[...]
    for batch in range(3):

        @pl.when(step // 2 == batch)
        def _():
            for i in range(0, 16, 2):
                outs[batch][:, i, :], outs[batch][:, i + 1, :] = two_planes(
                    in_ref[i], in_ref[i + 1], along_y, along_x
                )


def lateral_own(volume, along_y, along_x):
    square = pl.BlockSpec((256, 256), lambda i: (0, 0))

    def segment(batch):
        return pl.BlockSpec((PLANE, 16, PLANE), lambda i: (0, jnp.clip(i - 2 * batch, 0, 1), 0))

    return pl.pallas_call(
        own_body,
        grid=(6,),
        in_specs=[pl.BlockSpec((16, PLANE, PLANE), lambda i: (i, 0, 0)), square, square],
        out_specs=[segment(batch) for batch in range(3)],
        out_shape=[SEGMENT] * 3,
        name="blur_own",
        cost_estimate=cost(9),
        compiler_params=PARAMS,
    )(volume, along_y, along_x)


def pieces_body(sc_ref, *refs):
    pieces, (y_ref, x_ref, out_ref, held, sem) = refs[:8], refs[8:]
    copies = []
    for i, step in enumerate(STEP):
        chunk = lax.rem(sc_ref[0] + step, 4)
        for half in range(2):
            copies.append(
                pltpu.make_async_copy(
                    pieces[2 * i + half],
                    held.at[pl.ds(CHUNK * chunk, CHUNK), pl.ds(64 * half, 64)],
                    sem.at[2 * i + half],
                )
            )
            copies[-1].start()
    for copy in copies:
        copy.wait()
    along_y, along_x = y_ref[...], x_ref[...]
    for i in range(0, BATCH, 2):
        out_ref[:, i, :], out_ref[:, i + 1, :] = two_planes(held[i], held[i + 1], along_y, along_x)


def lateral_pieces(scalars, pieces, along_y, along_x):
    return pl.pallas_call(
        pieces_body,
        in_specs=[SCALARS] + [ANYWHERE] * 8 + [WHOLE] * 2,
        out_specs=WHOLE,
        out_shape=SEGMENT,
        scratch_shapes=[pltpu.VMEM((BATCH, PLANE, PLANE), F32), pltpu.SemaphoreType.DMA((8,))],
        name="blur_pieces",
        cost_estimate=cost(4),
        compiler_params=PARAMS,
    )(scalars, *[half for piece in pieces for half in piece], along_y, along_x)


def correct_body(
    batch, sc_ref, t0, t1, t2, d0, d1, w_ref, blur_ref, back_ref, y_ref, x_ref, *refs
):
    outs, returned = refs[:8], refs[8]
    step = pl.program_id(0)

    @pl.when(step < 16)
    def _():
        blur_z, return_z = blur_ref[...], back_ref[...]
        here = returned.at[:, pl.ds(pl.multiple_of(8 * lax.rem(step, 16), 8), 8), :]
        for y in range(0, 8, 2):
            high, low = zip(
                *[split(jnp.concatenate([t[y], t[y + 1]], 1)) for t in (t0, t1, t2)]
            )
            out = jnp.dot(
                blur_z, jnp.concatenate(high + low, 0), preferred_element_type=F32
            )
            blurred = out[: 2 * BATCH] + out[2 * BATCH :] + BACKGROUND
            data = jnp.concatenate(
                [
                    jnp.concatenate([d[0, :, y, :], d[0, :, y + 1, :]], 1)
                    for d in (d0, d1)
                ],
                0,
            )
            quotient = jnp.concatenate(split(data / blurred), 0)
            out = jnp.dot(return_z, quotient, preferred_element_type=F32)
            out = out[:BATCH] + out[BATCH:]
            here[:, y, :] = out[:, :PLANE]
            here[:, y + 1, :] = out[:, PLANE:]

    for which in range(4):

        @pl.when(step == 16 + which)
        def _():
            along_y, along_x = y_ref[...], x_ref[...]
            first = CHUNK * lax.rem(sc_ref[0] + STEP[which], 4)
            for i in range(0, CHUNK, 2):
                pair = two_planes(returned[first + i], returned[first + i + 1], along_y, along_x)
                for k in range(2):
                    value = pair[k] * w_ref[i + k]
                    inside = BATCH * batch + first + i + k >= sc_ref[1]
                    value = jnp.where(inside, value, 0.0)
                    outs[2 * which][i + k] = value[:64]
                    outs[2 * which + 1][i + k] = value[64:]


def chunk_at(step, sc):
    which = step - 16
    move = jnp.where(which <= 0, 2, jnp.where(which == 1, 1, jnp.where(which == 2, 3, 0)))
    return lax.rem(sc[0] + move, 4)


def correct(scalars, batch, segments, data, at, weights, operator):
    fixed = lambda m: pl.BlockSpec(m.shape, lambda i, sc: (0, 0))
    segment = pl.BlockSpec((8, BATCH, PLANE), lambda i, sc: (jnp.minimum(i, 15), 0, 0))
    rows = lambda k: pl.BlockSpec(
        (1, BATCH, 8, PLANE), lambda i, sc: (at + k, 0, jnp.minimum(i, 15), 0)
    )
    weight = pl.BlockSpec(
        (CHUNK, PLANE, PLANE),
        lambda i, sc: (BATCH // CHUNK * batch + chunk_at(i, sc), 0, 0),
    )
    matrices = operator[4], operator[5], operator[2], operator[3]
    return pl.pallas_call(
        functools.partial(correct_body, batch),
        grid_spec=pltpu.PrefetchScalarGridSpec(
            num_scalar_prefetch=1,
            grid=(20,),
            in_specs=[segment] * 3 + [rows(0), rows(1), weight] + [fixed(m) for m in matrices],
            out_specs=[pl.BlockSpec(PIECE.shape, lambda i, sc: (0, 0, 0))] * 8,
            scratch_shapes=[pltpu.VMEM((BATCH, PLANE, PLANE), F32)],
        ),
        out_shape=[PIECE] * 8,
        name="correct_batch",
        cost_estimate=cost(11),
        compiler_params=PARAMS,
    )(scalars, *segments, data, data, weights, *matrices)


def window_body(sc_ref, low, middle, high, out, held, sem):
    copies = [
        pltpu.make_async_copy(part, held.at[pl.ds(row, part.shape[0])], sem.at[i])
        for i, (part, row) in enumerate(((low, 0), (middle, 32), (high, 128)))
    ]
    for copy in copies:
        copy.start()
    for copy in copies:
        copy.wait()
    copy = pltpu.make_async_copy(held.at[pl.ds(sc_ref[2], 128)], out, sem.at[0])
    copy.start()
    copy.wait()


def window(scalars, low, middle, high):
    return pl.pallas_call(
        window_body,
        in_specs=[SCALARS] + [ANYWHERE] * 3,
        out_specs=ANYWHERE,
        out_shape=jax.ShapeDtypeStruct((128, PLANE, PLANE), F32),
        scratch_shapes=[pltpu.VMEM((144, PLANE, PLANE), F32), pltpu.SemaphoreType.DMA((3,))],
        name="data_window",
        cost_estimate=cost(5),
        compiler_params=PARAMS,
    )(scalars, low, middle, high)


def pick_body(steps, sc_ref, w_ref, *refs):
    outs, held, sem, out_sem = refs[:-3], refs[-3], refs[-2], refs[-1]
    reads, writes = [], []
    for i, step in enumerate(steps):
        chunk = lax.rem(sc_ref[0] + step, 4)
        for batch in range(3):
            reads.append(
                pltpu.make_async_copy(
                    w_ref.at[pl.ds(BATCH * batch + CHUNK * chunk, CHUNK)],
                    held.at[i, pl.ds(CHUNK * batch, CHUNK)],
                    sem.at[3 * i + batch],
                )
            )
            reads[-1].start()
    for i in range(len(steps)):
        for copy in reads[3 * i : 3 * i + 3]:
            copy.wait()
        for half in range(2):
            writes.append(
                pltpu.make_async_copy(
                    held.at[i, :, pl.ds(64 * half, 64)],
                    outs[2 * i + half],
                    out_sem.at[2 * i + half],
                )
            )
            writes[-1].start()
    for copy in writes:
        copy.wait()


def pick(scalars, volume, steps):
    rows = 3 * CHUNK
    return pl.pallas_call(
        functools.partial(pick_body, steps),
        in_specs=[SCALARS, ANYWHERE],
        out_specs=[ANYWHERE] * (2 * len(steps)),
        out_shape=[jax.ShapeDtypeStruct((rows, 64, PLANE), F32)] * (2 * len(steps)),
        scratch_shapes=[
            pltpu.VMEM((len(steps), rows, PLANE, PLANE), F32),
            pltpu.SemaphoreType.DMA((3 * len(steps),)),
            pltpu.SemaphoreType.DMA((2 * len(steps),)),
        ],
        name="pick_chunks",
        cost_estimate=cost(1.4 * len(steps)),
        compiler_params=PARAMS,
    )(scalars, volume)


def assemble_body(batch, sc_ref, *refs):
    pieces, (out, held, sem, out_sem) = refs[:8], refs[-4:]
    reads, writes = [], []
    for i, step in enumerate(STEP):
        row = CHUNK * lax.rem(sc_ref[0] + step, 4)
        spot = held.at[i]
        for half in range(2):
            reads.append(
                pltpu.make_async_copy(
                    pieces[2 * i + half], spot.at[:, pl.ds(64 * half, 64)], sem.at[2 * i + half]
                )
            )
            reads[-1].start()
        writes.append(
            pltpu.make_async_copy(
                spot, out.at[pl.ds(BATCH * batch + row, CHUNK)], out_sem.at[i]
            )
        )
    for i in range(4):
        reads[2 * i].wait()
        reads[2 * i + 1].wait()
        writes[i].start()
    for copy in writes:
        copy.wait()


def assemble(scalars, batch, pieces, whole):
    earlier = [] if whole is None else [whole]
    return pl.pallas_call(
        functools.partial(assemble_body, batch),
        in_specs=[SCALARS] + [ANYWHERE] * (8 + len(earlier)),
        out_specs=ANYWHERE,
        out_shape=jax.ShapeDtypeStruct((BLOCK, PLANE, PLANE), F32),
        scratch_shapes=[
            pltpu.VMEM((4, CHUNK, PLANE, PLANE), F32),
            pltpu.SemaphoreType.DMA((8,)),
            pltpu.SemaphoreType.DMA((4,)),
        ],
        input_output_aliases={9: 0} if earlier else {},
        name="assemble",
        cost_estimate=cost(2.5),
        compiler_params=PARAMS,
    )(scalars, *[half for piece in pieces for half in piece], *earlier)


def to_plus(value):
    return lax.ppermute(value, "view", [(i, (i + 1) % 4) for i in range(4)])


def to_minus(value):
    return lax.ppermute(value, "view", [(i, (i - 1) % 4) for i in range(4)])


def to_space(value, steps):
    count = lax.axis_size("space")
    pairs = [(i, i + steps) for i in range(count) if 0 <= i + steps < count]
    return lax.ppermute(value, "space", pairs)


def ring_sum(pieces):
    far_a = to_plus(pieces[0])
    far_b = to_minus(pieces[1])
    left_b = to_plus(pieces[3])
    right_a = to_minus(pieces[4])
    left_a = to_plus(pieces[2] + far_a)
    right_b = to_minus(pieces[5] + far_b)
    return pieces[6] + left_a + right_a, pieces[7] + left_b + right_b


def ring_gather(own):
    own_a, own_b = own
    left_a, right_b = to_plus(own_a), to_minus(own_b)
    left_b, right_a = to_plus(own_b), to_minus(own_a)
    far_a, far_b = to_plus(left_a), to_minus(right_b)
    return [(far_a, far_b), (right_a, right_b), (left_a, left_b), (own_a, own_b)]


def on_device(estimate, view_data, blend_weights, kernels, shifts):
    view, place = lax.axis_index("view"), lax.axis_index("space")
    shift = shifts[0]
    scalars = jnp.stack([view, jnp.where(place == 0, shift, 0), 16 - shift]).astype(jnp.int32)
    data, weights = view_data[0], blend_weights[0]
    operator = operators(kernels[0])

    picked = pick(scalars, weights, STEP)
    data, *picked = lax.optimization_barrier((data, *picked))
    weight_sum = ring_sum(picked)
    data_low = to_space(data[BLOCK - 32 :], 1)
    data_high = to_space(data[:16], -1)
    inner_data = lax.dynamic_slice_in_dim(data, 16 - shift, 64, 0).reshape(2, 32, PLANE, PLANE)
    own = pick(scalars, estimate, (0,))
    own = [[half[CHUNK * b : CHUNK * b + CHUNK] for half in own] for b in range(3)]
    weight_sum = [[half[CHUNK * b : CHUNK * b + CHUNK] for half in weight_sum] for b in range(3)]

    segments = list(lateral_own(estimate, operator[0], operator[1]))
    data = window(scalars, data_low, data, data_high).reshape(4, 32, PLANE, PLANE)
    whole = None
    for iteration in range(ITERS):
        rim_low, rim_high = to_space(segments[2], 1), to_space(segments[0], -1)
        line = [rim_low, *segments, rim_high]
        order = (1, 0, 2) if iteration == 0 else (1, 2, 0)
        for batch in order:
            early = iteration == 0 and batch == 1
            pieces = correct(
                scalars, batch, line[batch : batch + 3], inner_data if early else data,
                0 if early else batch, weights, operator,
            )
            total = ring_sum(pieces)
            own[batch] = [e * c / w for e, c, w in zip(own[batch], total, weight_sum[batch])]
            gathered = ring_gather(own[batch])
            if iteration == ITERS - 1:
                whole = assemble(scalars, batch, gathered, whole)
            else:
                segments[batch] = lateral_pieces(scalars, gathered, operator[0], operator[1])
    return whole


def solution(mesh):
    return jax.shard_map(
        on_device,
        mesh=mesh,
        in_specs=(
            P("space", None, None),
            P("view", "space", None, None),
            P("view", "space", None, None),
            P("view", None, None),
            P("view"),
        ),
        out_specs=P("space", None, None),
        check_vma=False,
    )
```

```python
import functools

import jax
import jax.numpy as jnp
from jax import lax
from jax.experimental import pallas as pl
from jax.experimental.pallas import tpu as pltpu
from jax.sharding import PartitionSpec as P

F32, BF16 = jnp.float32, jnp.bfloat16
ITERS = 2
BACKGROUND = 0.1
BLOCK = 96
BATCH = 32
QUARTERS = 4
CHUNK = 8
PLANE = 128
VMEM = 50 << 20
STEP = (2, 1, 3, 0)


def halves(m):
    high = lax.reduce_precision(m, 8, 7)
    return high.astype(BF16), (m - high).astype(BF16)


def split(value):
    high = value.astype(BF16)
    return high, (value - high.astype(F32)).astype(BF16)


def band(taps, rows, cols, index):
    tap = index(jnp.arange(rows)[:, None], jnp.arange(cols)[None, :])
    return jnp.sum(jnp.where(tap[:, :, None] == jnp.arange(taps.shape[0]), taps, 0.0), -1)


def left(m):
    high, low = halves(m)
    return jnp.block([[high, high], [low, jnp.zeros_like(low)]])


def right(m):
    high, low = halves(m)
    return jnp.block([[high, low], [high, jnp.zeros_like(low)]])


def twice(m):
    none = jnp.zeros_like(m)
    return jnp.block([[m, none], [none, m]])


def operators(kernels):
    k = kernels / jnp.sum(kernels, axis=1, keepdims=True)
    along_y = band(k[1], PLANE, PLANE, lambda a, b: a - b + 15)
    along_x = band(k[2], PLANE, PLANE, lambda a, b: a - b + 15)
    blur_z = band(k[0], 2 * BATCH, 3 * BATCH, lambda row, col: 31 - (col - row))
    return_z = band(k[0], BATCH, 2 * BATCH, lambda row, col: col - row - 1)
    return (
        left(along_y), right(along_x.T), left(along_y.T), right(along_x),
        left(blur_z), twice(left(return_z)),
    )


def cost(us):
    return pl.CostEstimate(flops=int(us * 1.15e9), bytes_accessed=0, transcendentals=0)


PARAMS = pltpu.CompilerParams(vmem_limit_bytes=VMEM)
ANYWHERE = pl.BlockSpec(memory_space=pl.ANY)
WHOLE = pl.BlockSpec(memory_space=pltpu.VMEM)
SCALARS = pl.BlockSpec(memory_space=pltpu.SMEM)
SEGMENT = jax.ShapeDtypeStruct((PLANE, BATCH, PLANE), F32)
PIECE = jax.ShapeDtypeStruct((CHUNK, PLANE // 2, PLANE), F32)


def two_planes(first, second, along_y, along_x):
    h0, l0 = split(first)
    h1, l1 = split(second)
    planes = jnp.concatenate(
        [jnp.concatenate([h0, h1], 1), jnp.concatenate([l0, l1], 1)], 0
    )
    out = jnp.dot(along_y, planes, preferred_element_type=F32)
    high, low = split(out[:PLANE] + out[PLANE:])
    rows = jnp.concatenate(
        [
            jnp.concatenate([high[:, :PLANE], low[:, :PLANE]], 1),
            jnp.concatenate([high[:, PLANE:], low[:, PLANE:]], 1),
        ],
        0,
    )
    out = jnp.dot(rows, along_x, preferred_element_type=F32)
    out = out[:, :PLANE] + out[:, PLANE:]
    return out[:PLANE], out[PLANE:]


def own_body(in_hbm, y_ref, x_ref, *refs):
    outs, (held, out, sem, out_sem) = refs[:3], refs[3:]
    reads = []
    for i in range(6):
        rows = pl.ds(16 * i, 16)
        reads.append(pltpu.make_async_copy(in_hbm.at[rows], held.at[rows], sem.at[i]))
        reads[-1].start()
    along_y, along_x = y_ref[...], x_ref[...]
    writes = []
    for batch in range(3):
        for i in range(BATCH // 2):
            if i % 8 == 0:
                reads[2 * batch + i // 8].wait()
            row = BATCH * batch + 2 * i
            out[batch, :, 2 * i, :], out[batch, :, 2 * i + 1, :] = two_planes(
                held[row], held[row + 1], along_y, along_x
            )
        writes.append(pltpu.make_async_copy(out.at[batch], outs[batch], out_sem.at[batch]))
        writes[-1].start()
    for copy in writes:
        copy.wait()


def lateral_own(volume, along_y, along_x):
    return pl.pallas_call(
        own_body,
        in_specs=[ANYWHERE] + [WHOLE] * 2,
        out_specs=[ANYWHERE] * 3,
        out_shape=[SEGMENT] * 3,
        scratch_shapes=[
            pltpu.VMEM((BLOCK, PLANE, PLANE), F32),
            pltpu.VMEM((3, PLANE, BATCH, PLANE), F32),
            pltpu.SemaphoreType.DMA((6,)),
            pltpu.SemaphoreType.DMA((3,)),
        ],
        name="blur_own",
        cost_estimate=cost(7),
        compiler_params=PARAMS,
    )(volume, along_y, along_x)


def pieces_body(sc_ref, *refs):
    pieces, (y_ref, x_ref, out_ref, held, sem) = refs[:8], refs[8:]
    copies = []
    for i, step in enumerate(STEP):
        chunk = lax.rem(sc_ref[0] + step, 4)
        for half in range(2):
            copies.append(
                pltpu.make_async_copy(
                    pieces[2 * i + half],
                    held.at[pl.ds(CHUNK * chunk, CHUNK), pl.ds(64 * half, 64)],
                    sem.at[2 * i + half],
                )
            )
            copies[-1].start()
    for copy in copies:
        copy.wait()
    along_y, along_x = y_ref[...], x_ref[...]
    for i in range(0, BATCH, 2):
        out_ref[:, i, :], out_ref[:, i + 1, :] = two_planes(held[i], held[i + 1], along_y, along_x)


def lateral_pieces(scalars, pieces, along_y, along_x):
    return pl.pallas_call(
        pieces_body,
        in_specs=[SCALARS] + [ANYWHERE] * 8 + [WHOLE] * 2,
        out_specs=WHOLE,
        out_shape=SEGMENT,
        scratch_shapes=[pltpu.VMEM((BATCH, PLANE, PLANE), F32), pltpu.SemaphoreType.DMA((8,))],
        name="blur_pieces",
        cost_estimate=cost(4),
        compiler_params=PARAMS,
    )(scalars, *[half for piece in pieces for half in piece], along_y, along_x)


def correct_body(batch, data_rows, sc_ref, *refs):
    count = len(data_rows)
    parts, datas = refs[:3], refs[3 : 3 + count]
    w_hbm, blur_ref, back_ref, y_ref, x_ref = refs[3 + count : 8 + count]
    outs, (t, d, w, returned, made, sem, out_sem) = refs[8 + count : 16 + count], refs[16 + count :]
    start = sc_ref[2]
    quarter = PLANE // QUARTERS
    reads = []
    for q in range(QUARTERS):
        side = pl.ds(quarter * q, quarter)
        now = [pltpu.make_async_copy(parts[i].at[side], t.at[i, side], sem.at[q, i]) for i in range(3)]
        for i, (row, rows, at) in enumerate(data_rows):
            now.append(
                pltpu.make_async_copy(
                    datas[i].at[pl.ds(row, rows), side], d.at[pl.ds(at, rows), side], sem.at[q, 3 + i]
                )
            )
        for copy in now:
            copy.start()
        reads.append(now)
    weight_copy = pltpu.make_async_copy(
        w_hbm.at[pl.ds(BATCH * batch, BATCH)], w, sem.at[QUARTERS, 0]
    )
    weight_copy.start()

    def quotient_of(y):
        high, low = zip(
            *[split(jnp.concatenate([t[i, y], t[i, y + 1]], 1)) for i in range(3)]
        )
        out = jnp.dot(blur_ref[...], jnp.concatenate(high + low, 0), preferred_element_type=F32)
        blurred = out[: 2 * BATCH] + out[2 * BATCH :] + BACKGROUND
        here = pl.ds(start, 2 * BATCH)
        data = jnp.concatenate([d[here, y, :], d[here, y + 1, :]], 1)
        return split(data / blurred)

    def rows_of(y):
        quotients = quotient_of(y) + quotient_of(y + 2)
        out = jnp.dot(
            back_ref[...], jnp.concatenate(quotients, 0), preferred_element_type=F32
        )
        for k in range(2):
            value = out[2 * BATCH * k :][:BATCH] + out[2 * BATCH * k + BATCH :][:BATCH]
            returned[:, y + 2 * k, :] = value[:, :PLANE]
            returned[:, y + 2 * k + 1, :] = value[:, PLANE:]

    for q in range(QUARTERS):
        for copy in reads[q]:
            copy.wait()

        @pl.loop(0, quarter // 32)
        def _(i):
            first = pl.multiple_of(quarter * q + 32 * i, 32)
            for y in range(0, 32, 4):
                rows_of(first + y)

    weight_copy.wait()
    along_y, along_x = y_ref[...], x_ref[...]
    writes = []
    for which, step in enumerate(STEP):
        first = CHUNK * lax.rem(sc_ref[0] + step, 4)
        for i in range(0, CHUNK, 2):
            pair = two_planes(returned[first + i], returned[first + i + 1], along_y, along_x)
            for k in range(2):
                value = pair[k] * w[first + i + k]
                inside = BATCH * batch + first + i + k >= sc_ref[1]
                made[which, i + k] = jnp.where(inside, value, 0.0)
        for half in range(2):
            writes.append(
                pltpu.make_async_copy(
                    made.at[which, :, pl.ds(64 * half, 64)],
                    outs[2 * which + half],
                    out_sem.at[2 * which + half],
                )
            )
            writes[-1].start()
    for copy in writes:
        copy.wait()


def correct(scalars, batch, segments, data, weights, operator):
    low, own, high = data
    chosen = (
        ((low, 0, 32, 0), (own, 0, 48, 32)),
        ((own, 0, 80, 0),),
        ((own, 32, 64, 0), (high, 0, 16, 64)),
    )[batch]
    return pl.pallas_call(
        functools.partial(correct_body, batch, [rows[1:] for rows in chosen]),
        in_specs=[SCALARS] + [ANYWHERE] * (4 + len(chosen)) + [WHOLE] * 4,
        out_specs=[ANYWHERE] * 8,
        out_shape=[PIECE] * 8,
        scratch_shapes=[
            pltpu.VMEM((3, PLANE, BATCH, PLANE), F32),
            pltpu.VMEM((80, PLANE, PLANE), F32),
            pltpu.VMEM((BATCH, PLANE, PLANE), F32),
            pltpu.VMEM((BATCH, PLANE, PLANE), F32),
            pltpu.VMEM((4, CHUNK, PLANE, PLANE), F32),
            pltpu.SemaphoreType.DMA((QUARTERS + 1, 5)),
            pltpu.SemaphoreType.DMA((8,)),
        ],
        name="correct_batch",
        cost_estimate=cost(12),
        compiler_params=PARAMS,
    )(
        scalars, *segments, *[rows[0] for rows in chosen], weights,
        operator[4], operator[5], operator[2], operator[3],
    )


def pick_body(steps, sc_ref, w_ref, *refs):
    outs, held, sem, out_sem = refs[:-3], refs[-3], refs[-2], refs[-1]
    reads, writes = [], []
    for i, step in enumerate(steps):
        chunk = lax.rem(sc_ref[0] + step, 4)
        for batch in range(3):
            reads.append(
                pltpu.make_async_copy(
                    w_ref.at[pl.ds(BATCH * batch + CHUNK * chunk, CHUNK)],
                    held.at[i, pl.ds(CHUNK * batch, CHUNK)],
                    sem.at[3 * i + batch],
                )
            )
            reads[-1].start()
    for i in range(len(steps)):
        for copy in reads[3 * i : 3 * i + 3]:
            copy.wait()
        for half in range(2):
            writes.append(
                pltpu.make_async_copy(
                    held.at[i, :, pl.ds(64 * half, 64)],
                    outs[2 * i + half],
                    out_sem.at[2 * i + half],
                )
            )
            writes[-1].start()
    for copy in writes:
        copy.wait()


def pick(scalars, volume, steps):
    rows = 3 * CHUNK
    return pl.pallas_call(
        functools.partial(pick_body, steps),
        in_specs=[SCALARS, ANYWHERE],
        out_specs=[ANYWHERE] * (2 * len(steps)),
        out_shape=[jax.ShapeDtypeStruct((rows, 64, PLANE), F32)] * (2 * len(steps)),
        scratch_shapes=[
            pltpu.VMEM((len(steps), rows, PLANE, PLANE), F32),
            pltpu.SemaphoreType.DMA((3 * len(steps),)),
            pltpu.SemaphoreType.DMA((2 * len(steps),)),
        ],
        name="pick_chunks",
        cost_estimate=cost(1.4 * len(steps)),
        compiler_params=PARAMS,
    )(scalars, volume)


def by_chunk_body(in_ref, out_ref):
    out_ref[...] = in_ref[...]


def by_chunk(volume):
    spec = lambda at: pl.BlockSpec((CHUNK, PLANE, PLANE), at)
    return pl.pallas_call(
        by_chunk_body,
        grid=(12,),
        in_specs=[spec(lambda i: (i % 3 * 4 + i // 3, 0, 0))],
        out_specs=spec(lambda i: (i, 0, 0)),
        out_shape=jax.ShapeDtypeStruct(volume.shape, F32),
        name="by_chunk",
        cost_estimate=cost(5),
        compiler_params=PARAMS,
    )(volume)


def assemble_body(batch, sc_ref, *refs):
    pieces, (out, held, sem, out_sem) = refs[:8], refs[-4:]
    reads, writes = [], []
    for i, step in enumerate(STEP):
        row = CHUNK * lax.rem(sc_ref[0] + step, 4)
        spot = held.at[i]
        for half in range(2):
            reads.append(
                pltpu.make_async_copy(
                    pieces[2 * i + half], spot.at[:, pl.ds(64 * half, 64)], sem.at[2 * i + half]
                )
            )
            reads[-1].start()
        writes.append(
            pltpu.make_async_copy(
                spot, out.at[pl.ds(BATCH * batch + row, CHUNK)], out_sem.at[i]
            )
        )
    for i in range(4):
        reads[2 * i].wait()
        reads[2 * i + 1].wait()
        writes[i].start()
    for copy in writes:
        copy.wait()


def assemble(scalars, batch, pieces, whole):
    earlier = [] if whole is None else [whole]
    return pl.pallas_call(
        functools.partial(assemble_body, batch),
        in_specs=[SCALARS] + [ANYWHERE] * (8 + len(earlier)),
        out_specs=ANYWHERE,
        out_shape=jax.ShapeDtypeStruct((BLOCK, PLANE, PLANE), F32),
        scratch_shapes=[
            pltpu.VMEM((4, CHUNK, PLANE, PLANE), F32),
            pltpu.SemaphoreType.DMA((8,)),
            pltpu.SemaphoreType.DMA((4,)),
        ],
        input_output_aliases={9: 0} if earlier else {},
        name="assemble",
        cost_estimate=cost(2.5),
        compiler_params=PARAMS,
    )(scalars, *[half for piece in pieces for half in piece], *earlier)


def to_plus(value):
    return lax.ppermute(value, "view", [(i, (i + 1) % 4) for i in range(4)])


def to_minus(value):
    return lax.ppermute(value, "view", [(i, (i - 1) % 4) for i in range(4)])


def to_space(value, steps):
    count = lax.axis_size("space")
    pairs = [(i, i + steps) for i in range(count) if 0 <= i + steps < count]
    return lax.ppermute(value, "space", pairs)


def ring_sum(pieces):
    far_a = to_plus(pieces[0])
    far_b = to_minus(pieces[1])
    left_b = to_plus(pieces[3])
    right_a = to_minus(pieces[4])
    left_a = to_plus(pieces[2] + far_a)
    right_b = to_minus(pieces[5] + far_b)
    return pieces[6] + left_a + right_a, pieces[7] + left_b + right_b


def ring_gather(own):
    own_a, own_b = own
    left_a, right_b = to_plus(own_a), to_minus(own_b)
    left_b, right_a = to_plus(own_b), to_minus(own_a)
    far_a, far_b = to_plus(left_a), to_minus(right_b)
    return [(far_a, far_b), (right_a, right_b), (left_a, left_b), (own_a, own_b)]


def on_device(estimate, view_data, blend_weights, kernels, shifts):
    view, place = lax.axis_index("view"), lax.axis_index("space")
    shift = shifts[0]
    scalars = jnp.stack([view, jnp.where(place == 0, shift, 0), 16 - shift]).astype(jnp.int32)
    data, weights = view_data[0], blend_weights[0]
    operator = operators(kernels[0])

    weight_sum = lax.psum_scatter(by_chunk(weights), "view", scatter_dimension=0, tiled=True)
    data = to_space(data[BLOCK - 32 :], 1), data, to_space(data[:16], -1)
    own = pick(scalars, estimate, (0,))
    own = [[half[CHUNK * b : CHUNK * b + CHUNK] for half in own] for b in range(3)]
    weight_sum = [
        [weight_sum[CHUNK * b : CHUNK * b + CHUNK, side] for side in (slice(0, 64), slice(64, 128))]
        for b in range(3)
    ]

    segments = list(lateral_own(estimate, operator[0], operator[1]))
    whole = None
    for iteration in range(ITERS):
        rim_low, rim_high = to_space(segments[2], 1), to_space(segments[0], -1)
        line = [rim_low, *segments, rim_high]
        order = (1, 0, 2) if iteration == 0 else (1, 2, 0)
        for batch in order:
            pieces = correct(scalars, batch, line[batch : batch + 3], data, weights, operator)
            total = ring_sum(pieces)
            own[batch] = [e * c / w for e, c, w in zip(own[batch], total, weight_sum[batch])]
            gathered = ring_gather(own[batch])
            if iteration == ITERS - 1:
                whole = assemble(scalars, batch, gathered, whole)
            else:
                segments[batch] = lateral_pieces(scalars, gathered, operator[0], operator[1])
    return whole


def solution(mesh):
    return jax.shard_map(
        on_device,
        mesh=mesh,
        in_specs=(
            P("space", None, None),
            P("view", "space", None, None),
            P("view", "space", None, None),
            P("view", None, None),
            P("view"),
        ),
        out_specs=P("space", None, None),
        check_vma=False,
    )
```

```python
import functools

import jax
import jax.numpy as jnp
from jax import lax
from jax.experimental import pallas as pl
from jax.experimental.pallas import tpu as pltpu
from jax.sharding import PartitionSpec as P

F32, BF16 = jnp.float32, jnp.bfloat16
ITERS = 2
BACKGROUND = 0.1
BLOCK = 96
BATCH = 32
QUARTERS = 4
CHUNK = 8
PLANE = 128
VMEM = 50 << 20
FIRST, OTHER, SECOND, OWN = range(4)
CHUNKS = 3


def halves(m):
    high = lax.reduce_precision(m, 8, 7)
    return high.astype(BF16), (m - high).astype(BF16)


def split(value):
    high = value.astype(BF16)
    return high, (value - high.astype(F32)).astype(BF16)


def band(taps, rows, cols, index):
    tap = index(jnp.arange(rows)[:, None], jnp.arange(cols)[None, :])
    return jnp.sum(jnp.where(tap[:, :, None] == jnp.arange(taps.shape[0]), taps, 0.0), -1)


def left(m):
    high, low = halves(m)
    return jnp.block([[high, high], [low, jnp.zeros_like(low)]])


def right(m):
    high, low = halves(m)
    return jnp.block([[high, low], [high, jnp.zeros_like(low)]])


def twice(m):
    none = jnp.zeros_like(m)
    return jnp.block([[m, none], [none, m]])


def operators(kernels):
    k = kernels / jnp.sum(kernels, axis=1, keepdims=True)
    along_y = band(k[1], PLANE, PLANE, lambda a, b: a - b + 15)
    along_x = band(k[2], PLANE, PLANE, lambda a, b: a - b + 15)
    blur_z = band(k[0], 2 * BATCH, 3 * BATCH, lambda row, col: 31 - (col - row))
    return_z = band(k[0], BATCH, 2 * BATCH, lambda row, col: col - row - 1)
    return (
        left(along_y), right(along_x.T), left(along_y.T), right(along_x),
        left(blur_z), twice(left(return_z)),
    )


def cost(us):
    return pl.CostEstimate(flops=int(us * 1.15e9), bytes_accessed=0, transcendentals=0)


PARAMS = pltpu.CompilerParams(vmem_limit_bytes=VMEM)
ANYWHERE = pl.BlockSpec(memory_space=pl.ANY)
WHOLE = pl.BlockSpec(memory_space=pltpu.VMEM)
SCALARS = pl.BlockSpec(memory_space=pltpu.SMEM)
SEGMENT = jax.ShapeDtypeStruct((PLANE, BATCH, PLANE), F32)


def two_planes(first, second, along_y, along_x):
    h0, l0 = split(first)
    h1, l1 = split(second)
    planes = jnp.concatenate(
        [jnp.concatenate([h0, h1], 1), jnp.concatenate([l0, l1], 1)], 0
    )
    out = jnp.dot(along_y, planes, preferred_element_type=F32)
    high, low = split(out[:PLANE] + out[PLANE:])
    rows = jnp.concatenate(
        [
            jnp.concatenate([high[:, :PLANE], low[:, :PLANE]], 1),
            jnp.concatenate([high[:, PLANE:], low[:, PLANE:]], 1),
        ],
        0,
    )
    out = jnp.dot(rows, along_x, preferred_element_type=F32)
    out = out[:, :PLANE] + out[:, PLANE:]
    return out[:PLANE], out[PLANE:]


def own_body(in_hbm, y_ref, x_ref, *refs):
    outs, (held, out, sem, out_sem) = refs[-7:-4], refs[-4:]
    reads = []
    for i in range(6):
        rows = pl.ds(16 * i, 16)
        reads.append(pltpu.make_async_copy(in_hbm.at[rows], held.at[rows], sem.at[i]))
        reads[-1].start()
    along_y, along_x = y_ref[...], x_ref[...]
    writes = []
    for batch in range(3):
        for i in range(BATCH // 2):
            if i % 8 == 0:
                reads[2 * batch + i // 8].wait()
            row = BATCH * batch + 2 * i
            out[batch, :, 2 * i, :], out[batch, :, 2 * i + 1, :] = two_planes(
                held[row], held[row + 1], along_y, along_x
            )
        writes.append(pltpu.make_async_copy(out.at[batch], outs[batch], out_sem.at[batch]))
        writes[-1].start()
    for copy in writes:
        copy.wait()


def lateral_own(volume, along_y, along_x, after):
    return pl.pallas_call(
        own_body,
        in_specs=[ANYWHERE] + [WHOLE] * 2 + [ANYWHERE] * len(after),
        out_specs=[ANYWHERE] * 3,
        out_shape=[SEGMENT] * 3,
        scratch_shapes=[
            pltpu.VMEM((BLOCK, PLANE, PLANE), F32),
            pltpu.VMEM((3, PLANE, BATCH, PLANE), F32),
            pltpu.SemaphoreType.DMA((6,)),
            pltpu.SemaphoreType.DMA((3,)),
        ],
        name="blur_own",
        cost_estimate=cost(12),
        compiler_params=PARAMS,
    )(volume, along_y, along_x, *after)


def chunks_of(refs):
    pair, second, own = refs
    return pair.at[0], pair.at[1], second, own


def pieces_body(sc_ref, *refs):
    y_ref, x_ref, out_ref, held, sem = refs[3:]
    copies = []
    for which, piece in enumerate(chunks_of(refs[:3])):
        spot = pl.ds(CHUNK * sc_ref[CHUNKS + which], CHUNK)
        copies.append(pltpu.make_async_copy(piece, held.at[spot], sem.at[which]))
        copies[-1].start()
    for copy in copies:
        copy.wait()
    along_y, along_x = y_ref[...], x_ref[...]
    for i in range(0, BATCH, 2):
        out_ref[:, i, :], out_ref[:, i + 1, :] = two_planes(held[i], held[i + 1], along_y, along_x)


def lateral_pieces(scalars, pieces, along_y, along_x):
    return pl.pallas_call(
        pieces_body,
        in_specs=[SCALARS] + [ANYWHERE] * 3 + [WHOLE] * 2,
        out_specs=WHOLE,
        out_shape=SEGMENT,
        scratch_shapes=[pltpu.VMEM((BATCH, PLANE, PLANE), F32), pltpu.SemaphoreType.DMA((4,))],
        name="blur_pieces",
        cost_estimate=cost(20.0),
        compiler_params=PARAMS,
    )(scalars, *pieces, along_y, along_x)


def send_out(held, which, outs, sem):
    first, second, own = outs
    target = first.at[which] if which in (FIRST, OTHER) else second if which == SECOND else own
    copy = pltpu.make_async_copy(held, target, sem.at[which])
    copy.start()
    return [copy]


def messages(rows):
    one = jax.ShapeDtypeStruct((rows, PLANE, PLANE), F32)
    return [jax.ShapeDtypeStruct((2, rows, PLANE, PLANE), F32), one, one]


def correct_body(batch, data_rows, waits, sc_ref, *refs):
    count = len(data_rows)
    parts, datas = refs[:3], refs[3 : 3 + count]
    w_hbm, blur_ref, back_ref, y_ref, x_ref = refs[3 + count : 8 + count]
    outs = refs[8 + count + waits : 11 + count + waits]
    t, d, w, returned, made, sem, out_sem = refs[11 + count + waits :]
    start = sc_ref[2]
    quarter = PLANE // QUARTERS
    reads = []
    for q in range(QUARTERS):
        side = pl.ds(quarter * q, quarter)
        now = [pltpu.make_async_copy(parts[i].at[side], t.at[i, side], sem.at[q, i]) for i in range(3)]
        for i, (row, rows, at) in enumerate(data_rows):
            now.append(
                pltpu.make_async_copy(
                    datas[i].at[pl.ds(row, rows), side], d.at[pl.ds(at, rows), side], sem.at[q, 3 + i]
                )
            )
        for copy in now:
            copy.start()
        reads.append(now)
    weight_copy = pltpu.make_async_copy(
        w_hbm.at[pl.ds(BATCH * batch, BATCH)], w, sem.at[QUARTERS, 0]
    )
    weight_copy.start()

    def quotient_of(y):
        high, low = zip(
            *[split(jnp.concatenate([t[i, y], t[i, y + 1]], 1)) for i in range(3)]
        )
        out = jnp.dot(blur_ref[...], jnp.concatenate(high + low, 0), preferred_element_type=F32)
        blurred = out[: 2 * BATCH] + out[2 * BATCH :] + BACKGROUND
        here = pl.ds(start, 2 * BATCH)
        data = jnp.concatenate([d[here, y, :], d[here, y + 1, :]], 1)
        return split(data / blurred)

    def rows_of(y):
        quotients = quotient_of(y) + quotient_of(y + 2)
        out = jnp.dot(
            back_ref[...], jnp.concatenate(quotients, 0), preferred_element_type=F32
        )
        for k in range(2):
            value = out[2 * BATCH * k :][:BATCH] + out[2 * BATCH * k + BATCH :][:BATCH]
            returned[:, y + 2 * k, :] = value[:, :PLANE]
            returned[:, y + 2 * k + 1, :] = value[:, PLANE:]

    for q in range(QUARTERS):
        for copy in reads[q]:
            copy.wait()

        @pl.loop(0, quarter // 32)
        def _(i):
            first = pl.multiple_of(quarter * q + 32 * i, 32)
            for y in range(0, 32, 4):
                rows_of(first + y)

    weight_copy.wait()
    along_y, along_x = y_ref[...], x_ref[...]
    writes = []
    for which in range(4):
        first = CHUNK * sc_ref[CHUNKS + which]
        for i in range(0, CHUNK, 2):
            pair = two_planes(returned[first + i], returned[first + i + 1], along_y, along_x)
            for k in range(2):
                value = pair[k] * w[first + i + k]
                inside = BATCH * batch + first + i + k >= sc_ref[1]
                made[which, i + k] = jnp.where(inside, value, 0.0)
        writes += send_out(made.at[which], which, outs, out_sem)
    for copy in writes:
        copy.wait()


def correct(scalars, batch, segments, data, weights, operator, after=()):
    low, own, high = data
    chosen = (
        ((low, 0, 32, 0), (own, 0, 48, 32)),
        ((own, 0, 80, 0),),
        ((own, 32, 64, 0), (high, 0, 16, 64)),
    )[batch]
    return pl.pallas_call(
        functools.partial(correct_body, batch, [rows[1:] for rows in chosen], len(after)),
        in_specs=[SCALARS] + [ANYWHERE] * (4 + len(chosen)) + [WHOLE] * 4 + [ANYWHERE] * len(after),
        out_specs=[ANYWHERE] * 3,
        out_shape=messages(CHUNK),
        scratch_shapes=[
            pltpu.VMEM((3, PLANE, BATCH, PLANE), F32),
            pltpu.VMEM((80, PLANE, PLANE), F32),
            pltpu.VMEM((BATCH, PLANE, PLANE), F32),
            pltpu.VMEM((BATCH, PLANE, PLANE), F32),
            pltpu.VMEM((4, CHUNK, PLANE, PLANE), F32),
            pltpu.SemaphoreType.DMA((QUARTERS + 1, 5)),
            pltpu.SemaphoreType.DMA((4,)),
        ],
        name="correct_batch",
        cost_estimate=cost(12),
        compiler_params=PARAMS,
    )(
        scalars, *segments, *[rows[0] for rows in chosen], weights,
        operator[4], operator[5], operator[2], operator[3], *after,
    )


def pick_body(steps, sc_ref, w_ref, *refs):
    outs, held, sem, out_sem = refs[:-3], refs[-3], refs[-2], refs[-1]
    reads, writes = [], []
    for i, which in enumerate(steps):
        chunk = sc_ref[CHUNKS + which]
        for batch in range(3):
            reads.append(
                pltpu.make_async_copy(
                    w_ref.at[pl.ds(BATCH * batch + CHUNK * chunk, CHUNK)],
                    held.at[i, pl.ds(CHUNK * batch, CHUNK)],
                    sem.at[3 * i + batch],
                )
            )
            reads[-1].start()
    for i, which in enumerate(steps):
        for copy in reads[3 * i : 3 * i + 3]:
            copy.wait()
        if len(steps) == 4:
            writes += send_out(held.at[i], which, outs, out_sem)
        else:
            writes += send_out(held.at[i], which, [None] * 2 + list(outs), out_sem)
    for copy in writes:
        copy.wait()


def pick(scalars, volume, steps):
    rows = 3 * CHUNK
    outs = messages(rows) if len(steps) == 4 else messages(rows)[2:]
    return pl.pallas_call(
        functools.partial(pick_body, steps),
        in_specs=[SCALARS, ANYWHERE],
        out_specs=[ANYWHERE] * len(outs),
        out_shape=outs,
        scratch_shapes=[
            pltpu.VMEM((len(steps), rows, PLANE, PLANE), F32),
            pltpu.SemaphoreType.DMA((3 * len(steps),)),
            pltpu.SemaphoreType.DMA((8,)),
        ],
        name="pick_chunks",
        cost_estimate=cost(1.4 * len(steps)),
        compiler_params=PARAMS,
    )(scalars, volume)


def assemble_body(batch, sc_ref, *refs):
    out, held, sem, out_sem = refs[-4:]
    reads, writes = [], []
    for which, piece in enumerate(chunks_of(refs[:3])):
        row = BATCH * batch + CHUNK * sc_ref[CHUNKS + which]
        reads.append(pltpu.make_async_copy(piece, held.at[which], sem.at[which]))
        reads[-1].start()
        writes.append(
            pltpu.make_async_copy(held.at[which], out.at[pl.ds(row, CHUNK)], out_sem.at[which])
        )
    for read, write in zip(reads, writes):
        read.wait()
        write.start()
    for copy in writes:
        copy.wait()


def assemble(scalars, batch, pieces, whole):
    earlier = [] if whole is None else [whole]
    return pl.pallas_call(
        functools.partial(assemble_body, batch),
        in_specs=[SCALARS] + [ANYWHERE] * (3 + len(earlier)),
        out_specs=ANYWHERE,
        out_shape=jax.ShapeDtypeStruct((BLOCK, PLANE, PLANE), F32),
        scratch_shapes=[
            pltpu.VMEM((4, CHUNK, PLANE, PLANE), F32),
            pltpu.SemaphoreType.DMA((4,)),
            pltpu.SemaphoreType.DMA((4,)),
        ],
        input_output_aliases={4: 0} if earlier else {},
        name="assemble",
        cost_estimate=cost(2.5),
        compiler_params=PARAMS,
    )(scalars, *pieces, *earlier)


def elementwise_call(body, name, us, outs, args, after=()):
    def kernel(*refs):
        body(*refs[: len(args)], *refs[len(args) + len(after) :])

    return pl.pallas_call(
        kernel,
        in_specs=[WHOLE] * len(args) + [ANYWHERE] * len(after),
        out_specs=[WHOLE] * len(outs),
        out_shape=outs,
        name=name,
        cost_estimate=cost(us),
        compiler_params=PARAMS,
    )(*args, *after)


def add_body(second, arrived, out):
    out[...] = second[...] + arrived[1]


def update_body(estimate, own, arrived, last, weight, out):
    out[...] = estimate[...] * (own[...] + arrived[0] + last[...]) / weight[...]


def total_body(own, arrived, last, out):
    out[...] = own[...] + arrived[0] + last[...]


def join_body(own, second, out):
    out[0] = own[...]
    out[1] = second[...]


def like(array, *lead):
    return jax.ShapeDtypeStruct((*lead, *array.shape), F32)


def exchange(value, turn):
    count = lax.axis_size("space")
    pairs = []
    for view in range(4):
        for place in range(count):
            partner = view ^ (1, 3)[(place + turn) % 2]
            pairs.append((view * count + place, partner * count + place))
    return lax.ppermute(value, ("view", "space"), pairs)


def to_space(value, steps):
    count = lax.axis_size("space")
    pairs = [(i, i + steps) for i in range(count) if 0 <= i + steps < count]
    return lax.ppermute(value, "space", pairs)


def on_device(estimate, view_data, blend_weights, kernels, shifts):
    view, place = lax.axis_index("view"), lax.axis_index("space")
    shift = shifts[0]
    near = jnp.where(place % 2 == 0, 1, 3)
    scalars = jnp.stack(
        [
            view, jnp.where(place == 0, shift, 0), 16 - shift,
            view ^ near, view ^ 2, view ^ near ^ 2, view,
        ]
    ).astype(jnp.int32)
    data, weights = view_data[0], blend_weights[0]
    operator = operators(kernels[0])

    picked = pick(scalars, weights, range(4))
    weight_first = exchange(picked[0], 0)
    data = to_space(data[BLOCK - 32 :], 1), data, to_space(data[:16], -1)
    estimates = pick(scalars, estimate, (OWN,))[0]
    own = [estimates[CHUNK * b : CHUNK * b + CHUNK] for b in range(3)]
    segments = lateral_own(estimate, operator[0], operator[1], [picked[1], estimates])
    line = [to_space(segments[2], 1), *segments, to_space(segments[0], -1)]
    whole = weight_sum = None
    for iteration in range(ITERS):
        order = (1, 0, 2) if iteration == 0 else (1, 2, 0)
        message, first, added, last, back, gathered = {}, {}, {}, {}, {}, {}

        def compute(batch, after=()):
            message[batch] = correct(
                scalars, batch, line[batch : batch + 3], data, weights, operator, after
            )
            first[batch] = exchange(message[batch][0], 0)

        def add(batch, after=()):
            second = message[batch][1]
            (added[batch],) = elementwise_call(
                add_body, "add", 2, [like(second)], (second, first[batch]), after
            )
            last[batch] = exchange(added[batch], 1)

        def update(batch, after=()):
            (own[batch],) = elementwise_call(
                update_body, "update", 2, [like(own[batch])],
                (own[batch], message[batch][2], first[batch], last[batch], weight_sum[batch]),
                after,
            )
            back[batch] = exchange(own[batch], 1)

        def join(batch, after=()):
            (pair,) = elementwise_call(
                join_body, "join", 2, [like(own[batch], 2)], (own[batch], back[batch]), after
            )
            gathered[batch] = exchange(pair, 0), back[batch], own[batch]

        x, y, z = order
        early = iteration == 0
        if early:
            (weight_added,) = elementwise_call(
                add_body, "add", 3, [like(picked[1])], (picked[1], weight_first)
            )
            weight_last = exchange(weight_added, 1)
            (total,) = elementwise_call(
                total_body, "weight_total", 4, [like(picked[2])], (picked[2], weight_first, weight_last)
            )
            weight_sum = [total[CHUNK * b : CHUNK * b + CHUNK] for b in range(3)]
        compute(x, [weight_added] if early else ())
        compute(y, message[x][1:2])
        add(x, message[y][1:2])
        compute(z, [added[x]])
        add(y, message[z][1:2])
        update(x, [added[y]])
        add(z, [own[x]])
        update(y, [added[z]])
        join(x, [own[y]])
        update(z, [gathered[x][1]])
        join(y, [own[z]])
        join(z)
        if iteration == ITERS - 1:
            for batch in order:
                whole = assemble(scalars, batch, gathered[batch], whole)
            return whole
        segments = [None] * 3
        for batch in order:
            segments[batch] = lateral_pieces(scalars, gathered[batch], operator[0], operator[1])
        line = [to_space(segments[2], 1), *segments, to_space(segments[0], -1)]


def solution(mesh):
    return jax.shard_map(
        on_device,
        mesh=mesh,
        in_specs=(
            P("space", None, None),
            P("view", "space", None, None),
            P("view", "space", None, None),
            P("view", None, None),
            P("view"),
        ),
        out_specs=P("space", None, None),
        check_vma=False,
    )
```

```python
import functools

import jax
import jax.numpy as jnp
from jax import lax
from jax.experimental import pallas as pl
from jax.experimental.pallas import tpu as pltpu
from jax.sharding import PartitionSpec as P

F32, BF16 = jnp.float32, jnp.bfloat16
ITERS = 2
BACKGROUND = 0.1
BLOCK = 96
BATCH = 32
QUARTERS = 4
CHUNK = 8
PLANE = 128
VMEM = 50 << 20
FIRST, OTHER, SECOND, OWN = range(4)
CHUNKS = 3


def halves(m):
    high = lax.reduce_precision(m, 8, 7)
    return high.astype(BF16), (m - high).astype(BF16)


def split(value):
    high = value.astype(BF16)
    return high, (value - high.astype(F32)).astype(BF16)


def band(taps, rows, cols, index):
    tap = index(jnp.arange(rows)[:, None], jnp.arange(cols)[None, :])
    return jnp.sum(jnp.where(tap[:, :, None] == jnp.arange(taps.shape[0]), taps, 0.0), -1)


def left(m):
    high, low = halves(m)
    return jnp.block([[high, high], [low, jnp.zeros_like(low)]])


def right(m):
    high, low = halves(m)
    return jnp.block([[high, low], [high, jnp.zeros_like(low)]])


def twice(m):
    none = jnp.zeros_like(m)
    return jnp.block([[m, none], [none, m]])


def operators(kernels):
    k = kernels / jnp.sum(kernels, axis=1, keepdims=True)
    along_y = band(k[1], PLANE, PLANE, lambda a, b: a - b + 15)
    along_x = band(k[2], PLANE, PLANE, lambda a, b: a - b + 15)
    blur_z = band(k[0], 2 * BATCH, 3 * BATCH, lambda row, col: 31 - (col - row))
    return_z = band(k[0], BATCH, 2 * BATCH, lambda row, col: col - row - 1)
    return (
        left(along_y), right(along_x.T), left(along_y.T), right(along_x),
        left(blur_z), twice(left(return_z)),
    )


def cost(us):
    return pl.CostEstimate(flops=int(us * 1.15e9), bytes_accessed=0, transcendentals=0)


PARAMS = pltpu.CompilerParams(vmem_limit_bytes=VMEM)
ANYWHERE = pl.BlockSpec(memory_space=pl.ANY)
WHOLE = pl.BlockSpec(memory_space=pltpu.VMEM)
SCALARS = pl.BlockSpec(memory_space=pltpu.SMEM)
SEGMENT = jax.ShapeDtypeStruct((PLANE, BATCH, PLANE), F32)


def two_planes(first, second, along_y, along_x):
    h0, l0 = split(first)
    h1, l1 = split(second)
    planes = jnp.concatenate(
        [jnp.concatenate([h0, h1], 1), jnp.concatenate([l0, l1], 1)], 0
    )
    out = jnp.dot(along_y, planes, preferred_element_type=F32)
    high, low = split(out[:PLANE] + out[PLANE:])
    rows = jnp.concatenate(
        [
            jnp.concatenate([high[:, :PLANE], low[:, :PLANE]], 1),
            jnp.concatenate([high[:, PLANE:], low[:, PLANE:]], 1),
        ],
        0,
    )
    out = jnp.dot(rows, along_x, preferred_element_type=F32)
    out = out[:, :PLANE] + out[:, PLANE:]
    return out[:PLANE], out[PLANE:]


def own_body(in_hbm, y_ref, x_ref, *refs):
    outs, (held, out, sem, out_sem) = refs[-7:-4], refs[-4:]
    reads = []
    for i in range(6):
        rows = pl.ds(16 * i, 16)
        reads.append(pltpu.make_async_copy(in_hbm.at[rows], held.at[rows], sem.at[i]))
        reads[-1].start()
    along_y, along_x = y_ref[...], x_ref[...]
    writes = []
    for batch in range(3):
        for i in range(BATCH // 2):
            if i % 8 == 0:
                reads[2 * batch + i // 8].wait()
            row = BATCH * batch + 2 * i
            out[batch, :, 2 * i, :], out[batch, :, 2 * i + 1, :] = two_planes(
                held[row], held[row + 1], along_y, along_x
            )
        writes.append(pltpu.make_async_copy(out.at[batch], outs[batch], out_sem.at[batch]))
        writes[-1].start()
    for copy in writes:
        copy.wait()


def lateral_own(volume, along_y, along_x, after):
    return pl.pallas_call(
        own_body,
        in_specs=[ANYWHERE] + [WHOLE] * 2 + [ANYWHERE] * len(after),
        out_specs=[ANYWHERE] * 3,
        out_shape=[SEGMENT] * 3,
        scratch_shapes=[
            pltpu.VMEM((BLOCK, PLANE, PLANE), F32),
            pltpu.VMEM((3, PLANE, BATCH, PLANE), F32),
            pltpu.SemaphoreType.DMA((6,)),
            pltpu.SemaphoreType.DMA((3,)),
        ],
        name="blur_own",
        cost_estimate=cost(0.5),
        compiler_params=PARAMS,
    )(volume, along_y, along_x, *after)


def chunks_of(refs):
    pair, second, own = refs
    return pair.at[0], pair.at[1], second, own


def pieces_body(sc_ref, *refs):
    y_ref, x_ref, out_ref, held, sem = refs[3:]
    copies = []
    for which, piece in enumerate(chunks_of(refs[:3])):
        spot = pl.ds(CHUNK * sc_ref[CHUNKS + which], CHUNK)
        copies.append(pltpu.make_async_copy(piece, held.at[spot], sem.at[which]))
        copies[-1].start()
    for copy in copies:
        copy.wait()
    along_y, along_x = y_ref[...], x_ref[...]
    for i in range(0, BATCH, 2):
        out_ref[:, i, :], out_ref[:, i + 1, :] = two_planes(held[i], held[i + 1], along_y, along_x)


def lateral_pieces(scalars, pieces, along_y, along_x):
    return pl.pallas_call(
        pieces_body,
        in_specs=[SCALARS] + [ANYWHERE] * 3 + [WHOLE] * 2,
        out_specs=WHOLE,
        out_shape=SEGMENT,
        scratch_shapes=[pltpu.VMEM((BATCH, PLANE, PLANE), F32), pltpu.SemaphoreType.DMA((4,))],
        name="blur_pieces",
        cost_estimate=cost(0.5),
        compiler_params=PARAMS,
    )(scalars, *pieces, along_y, along_x)


def send_out(held, which, outs, sem):
    first, second, own = outs
    target = first.at[which] if which in (FIRST, OTHER) else second if which == SECOND else own
    copy = pltpu.make_async_copy(held, target, sem.at[which])
    copy.start()
    return [copy]


def messages(rows):
    one = jax.ShapeDtypeStruct((rows, PLANE, PLANE), F32)
    return [jax.ShapeDtypeStruct((2, rows, PLANE, PLANE), F32), one, one]


def correct_body(batch, data_rows, waits, sc_ref, *refs):
    count = len(data_rows)
    parts, datas = refs[:3], refs[3 : 3 + count]
    w_hbm, blur_ref, back_ref, y_ref, x_ref = refs[3 + count : 8 + count]
    outs = refs[8 + count + waits : 11 + count + waits]
    t, d, w, returned, made, sem, out_sem = refs[11 + count + waits :]
    start = sc_ref[2]
    quarter = PLANE // QUARTERS
    reads = []
    for q in range(QUARTERS):
        side = pl.ds(quarter * q, quarter)
        now = [pltpu.make_async_copy(parts[i].at[side], t.at[i, side], sem.at[q, i]) for i in range(3)]
        for i, (row, rows, at) in enumerate(data_rows):
            now.append(
                pltpu.make_async_copy(
                    datas[i].at[pl.ds(row, rows), side], d.at[pl.ds(at, rows), side], sem.at[q, 3 + i]
                )
            )
        for copy in now:
            copy.start()
        reads.append(now)
    weight_copy = pltpu.make_async_copy(
        w_hbm.at[pl.ds(BATCH * batch, BATCH)], w, sem.at[QUARTERS, 0]
    )
    weight_copy.start()

    def quotient_of(y):
        high, low = zip(
            *[split(jnp.concatenate([t[i, y], t[i, y + 1]], 1)) for i in range(3)]
        )
        out = jnp.dot(blur_ref[...], jnp.concatenate(high + low, 0), preferred_element_type=F32)
        blurred = out[: 2 * BATCH] + out[2 * BATCH :] + BACKGROUND
        here = pl.ds(start, 2 * BATCH)
        data = jnp.concatenate([d[here, y, :], d[here, y + 1, :]], 1)
        return split(data / blurred)

    def rows_of(y):
        quotients = quotient_of(y) + quotient_of(y + 2)
        out = jnp.dot(
            back_ref[...], jnp.concatenate(quotients, 0), preferred_element_type=F32
        )
        for k in range(2):
            value = out[2 * BATCH * k :][:BATCH] + out[2 * BATCH * k + BATCH :][:BATCH]
            returned[:, y + 2 * k, :] = value[:, :PLANE]
            returned[:, y + 2 * k + 1, :] = value[:, PLANE:]

    for q in range(QUARTERS):
        for copy in reads[q]:
            copy.wait()

        @pl.loop(0, quarter // 32)
        def _(i):
            first = pl.multiple_of(quarter * q + 32 * i, 32)
            for y in range(0, 32, 4):
                rows_of(first + y)

    weight_copy.wait()
    along_y, along_x = y_ref[...], x_ref[...]
    writes = []
    for which in range(4):
        first = CHUNK * sc_ref[CHUNKS + which]
        for i in range(0, CHUNK, 2):
            pair = two_planes(returned[first + i], returned[first + i + 1], along_y, along_x)
            for k in range(2):
                value = pair[k] * w[first + i + k]
                inside = BATCH * batch + first + i + k >= sc_ref[1]
                made[which, i + k] = jnp.where(inside, value, 0.0)
        writes += send_out(made.at[which], which, outs, out_sem)
    for copy in writes:
        copy.wait()


def correct(scalars, batch, segments, data, weights, operator, after=()):
    low, own, high = data
    chosen = (
        ((low, 0, 32, 0), (own, 0, 48, 32)),
        ((own, 0, 80, 0),),
        ((own, 32, 64, 0), (high, 0, 16, 64)),
    )[batch]
    return pl.pallas_call(
        functools.partial(correct_body, batch, [rows[1:] for rows in chosen], len(after)),
        in_specs=[SCALARS] + [ANYWHERE] * (4 + len(chosen)) + [WHOLE] * 4 + [ANYWHERE] * len(after),
        out_specs=[ANYWHERE] * 3,
        out_shape=messages(CHUNK),
        scratch_shapes=[
            pltpu.VMEM((3, PLANE, BATCH, PLANE), F32),
            pltpu.VMEM((80, PLANE, PLANE), F32),
            pltpu.VMEM((BATCH, PLANE, PLANE), F32),
            pltpu.VMEM((BATCH, PLANE, PLANE), F32),
            pltpu.VMEM((4, CHUNK, PLANE, PLANE), F32),
            pltpu.SemaphoreType.DMA((QUARTERS + 1, 5)),
            pltpu.SemaphoreType.DMA((4,)),
        ],
        name="correct_batch",
        cost_estimate=cost(0.5),
        compiler_params=PARAMS,
    )(
        scalars, *segments, *[rows[0] for rows in chosen], weights,
        operator[4], operator[5], operator[2], operator[3], *after,
    )


def pick_body(chosen, waits, sc_ref, volume, *refs):
    outs, (held, sem, out_sem) = refs[waits:-3], refs[-3:]
    targets = {FIRST: outs[0].at[0], OTHER: outs[0].at[1]} if FIRST in chosen else dict(zip(chosen, outs))
    reads, writes = [], []
    for i, which in enumerate(chosen):
        chunk = sc_ref[CHUNKS + which]
        for batch in range(3):
            reads.append(
                pltpu.make_async_copy(
                    volume.at[pl.ds(BATCH * batch + CHUNK * chunk, CHUNK)],
                    held.at[i, pl.ds(CHUNK * batch, CHUNK)],
                    sem.at[3 * i + batch],
                )
            )
            reads[-1].start()
    for i, which in enumerate(chosen):
        for copy in reads[3 * i : 3 * i + 3]:
            copy.wait()
        writes.append(pltpu.make_async_copy(held.at[i], targets[which], out_sem.at[i]))
        writes[-1].start()
    for copy in writes:
        copy.wait()


def pick(scalars, volume, chosen, after=()):
    rows = 3 * CHUNK
    pair, one, _ = messages(rows)
    outs = [pair] if FIRST in chosen else [one] * len(chosen)
    return pl.pallas_call(
        functools.partial(pick_body, chosen, len(after)),
        in_specs=[SCALARS, ANYWHERE] + [ANYWHERE] * len(after),
        out_specs=[ANYWHERE] * len(outs),
        out_shape=outs,
        scratch_shapes=[
            pltpu.VMEM((len(chosen), rows, PLANE, PLANE), F32),
            pltpu.SemaphoreType.DMA((3 * len(chosen),)),
            pltpu.SemaphoreType.DMA((len(chosen),)),
        ],
        name="pick_chunks",
        cost_estimate=cost(1.4 * len(chosen)),
        compiler_params=PARAMS,
    )(scalars, volume, *after)


def assemble_body(batch, sc_ref, *refs):
    out, held, sem, out_sem = refs[-4:]
    reads, writes = [], []
    for which, piece in enumerate(chunks_of(refs[:3])):
        row = BATCH * batch + CHUNK * sc_ref[CHUNKS + which]
        reads.append(pltpu.make_async_copy(piece, held.at[which], sem.at[which]))
        reads[-1].start()
        writes.append(
            pltpu.make_async_copy(held.at[which], out.at[pl.ds(row, CHUNK)], out_sem.at[which])
        )
    for read, write in zip(reads, writes):
        read.wait()
        write.start()
    for copy in writes:
        copy.wait()


def assemble(scalars, batch, pieces, whole):
    earlier = [] if whole is None else [whole]
    return pl.pallas_call(
        functools.partial(assemble_body, batch),
        in_specs=[SCALARS] + [ANYWHERE] * (3 + len(earlier)),
        out_specs=ANYWHERE,
        out_shape=jax.ShapeDtypeStruct((BLOCK, PLANE, PLANE), F32),
        scratch_shapes=[
            pltpu.VMEM((4, CHUNK, PLANE, PLANE), F32),
            pltpu.SemaphoreType.DMA((4,)),
            pltpu.SemaphoreType.DMA((4,)),
        ],
        input_output_aliases={4: 0} if earlier else {},
        name="assemble",
        cost_estimate=cost(0.5),
        compiler_params=PARAMS,
    )(scalars, *pieces, *earlier)


def elementwise_call(body, name, us, outs, args, after=()):
    def kernel(*refs):
        body(*refs[: len(args)], *refs[len(args) + len(after) :])

    return pl.pallas_call(
        kernel,
        in_specs=[WHOLE] * len(args) + [ANYWHERE] * len(after),
        out_specs=[WHOLE] * len(outs),
        out_shape=outs,
        name=name,
        cost_estimate=cost(0.5),
        compiler_params=PARAMS,
    )(*args, *after)


def add_body(second, arrived, out):
    out[...] = second[...] + arrived[1]


def update_body(estimate, own, arrived, last, weight, out):
    out[...] = estimate[...] * (own[...] + arrived[0] + last[...]) / weight[...]


def total_body(own, arrived, last, out):
    out[...] = own[...] + arrived[0] + last[...]


def join_body(own, second, out):
    out[0] = own[...]
    out[1] = second[...]


def like(array, *lead):
    return jax.ShapeDtypeStruct((*lead, *array.shape), F32)


def exchange(value, turn):
    count = lax.axis_size("space")
    pairs = []
    for view in range(4):
        for place in range(count):
            partner = view ^ (1, 3)[(place + turn) % 2]
            pairs.append((view * count + place, partner * count + place))
    return lax.ppermute(value, ("view", "space"), pairs)


def to_space(value, steps):
    count = lax.axis_size("space")
    pairs = [(i, i + steps) for i in range(count) if 0 <= i + steps < count]
    return lax.ppermute(value, "space", pairs)


def on_device(estimate, view_data, blend_weights, kernels, shifts):
    view, place = lax.axis_index("view"), lax.axis_index("space")
    shift = shifts[0]
    near = jnp.where(place % 2 == 0, 1, 3)
    scalars = jnp.stack(
        [
            view, jnp.where(place == 0, shift, 0), 16 - shift,
            view ^ near, view ^ 2, view ^ near ^ 2, view,
        ]
    ).astype(jnp.int32)
    data, weights = view_data[0], blend_weights[0]
    operator = operators(kernels[0])

    (first_weights,) = pick(scalars, weights, (FIRST, OTHER))
    weight_first = exchange(first_weights, 0)
    data, first_weights = lax.optimization_barrier((data, first_weights))
    sides = data[BLOCK - 32 :], data[:16]
    data = to_space(sides[0], 1), data, to_space(sides[1], -1)
    second_weights, own_weights = pick(scalars, weights, (SECOND, OWN), sides)
    (estimates,) = pick(scalars, estimate, (OWN,), sides)
    own = [estimates[CHUNK * b : CHUNK * b + CHUNK] for b in range(3)]
    segments = lateral_own(
        estimate, operator[0], operator[1], [first_weights, *sides, estimates, own_weights]
    )
    line = [to_space(segments[2], 1), *segments, to_space(segments[0], -1)]
    whole = weight_sum = None
    for iteration in range(ITERS):
        order = (1, 0, 2) if iteration == 0 else (1, 2, 0)
        message, first, added, last, back, gathered = {}, {}, {}, {}, {}, {}

        def compute(batch, after=()):
            message[batch] = correct(
                scalars, batch, line[batch : batch + 3], data, weights, operator, after
            )
            first[batch] = exchange(message[batch][0], 0)

        def add(batch, after=()):
            second = message[batch][1]
            (added[batch],) = elementwise_call(
                add_body, "add", 2, [like(second)], (second, first[batch]), after
            )
            last[batch] = exchange(added[batch], 1)

        def update(batch, after=()):
            (own[batch],) = elementwise_call(
                update_body, "update", 2, [like(own[batch])],
                (own[batch], message[batch][2], first[batch], last[batch], weight_sum[batch]),
                after,
            )
            back[batch] = exchange(own[batch], 1)

        def join(batch, after=()):
            (pair,) = elementwise_call(
                join_body, "join", 2, [like(own[batch], 2)], (own[batch], back[batch]), after
            )
            gathered[batch] = exchange(pair, 0), back[batch], own[batch]

        x, y, z = order
        early = iteration == 0
        if early:
            compute(x, [data[0], data[2]])
            (weight_added,) = elementwise_call(
                add_body, "add", 3, [like(second_weights)], (second_weights, weight_first), message[x][1:2]
            )
            weight_last = exchange(weight_added, 1)
            compute(y, [weight_added, line[0], line[4]])
            add(x, message[y][1:2])
            compute(z, [added[x]])
            (total,) = elementwise_call(
                total_body, "weight_total", 4, [like(own_weights)],
                (own_weights, weight_first, weight_last), message[z][1:2]
            )
            weight_sum = [total[CHUNK * b : CHUNK * b + CHUNK] for b in range(3)]
            add(y, [total])
        else:
            compute(x)
            compute(y, message[x][1:2])
            add(x, message[y][1:2])
            compute(z, [added[x]])
            add(y, message[z][1:2])
        update(x, [added[y]])
        add(z, [own[x]])
        update(y, [added[z]])
        join(x, [own[y]])
        update(z, [gathered[x][1]])
        join(y, [own[z]])
        join(z)
        if iteration == ITERS - 1:
            for batch in order:
                whole = assemble(scalars, batch, gathered[batch], whole)
            return whole
        segments = [None] * 3
        for batch in order:
            segments[batch] = lateral_pieces(scalars, gathered[batch], operator[0], operator[1])
        line = [to_space(segments[2], 1), *segments, to_space(segments[0], -1)]


def solution(mesh):
    return jax.shard_map(
        on_device,
        mesh=mesh,
        in_specs=(
            P("space", None, None),
            P("view", "space", None, None),
            P("view", "space", None, None),
            P("view", None, None),
            P("view"),
        ),
        out_specs=P("space", None, None),
        check_vma=False,
    )
```

```python
import functools

import jax
import jax.numpy as jnp
from jax import lax
from jax.experimental import pallas as pl
from jax.experimental.pallas import tpu as pltpu
from jax.sharding import PartitionSpec as P

F32, BF16 = jnp.float32, jnp.bfloat16
ITERS = 2
BACKGROUND = 0.1
BLOCK = 96
BATCH = 32
QUARTERS = 4
CHUNK = 8
PLANE = 128
VMEM = 50 << 20
FIRST, OTHER, SECOND, OWN = range(4)
CHUNKS = 3


def halves(m):
    high = lax.reduce_precision(m, 8, 7)
    return high.astype(BF16), (m - high).astype(BF16)


def split(value):
    high = value.astype(BF16)
    return high, (value - high.astype(F32)).astype(BF16)


def band(taps, rows, cols, index):
    tap = index(jnp.arange(rows)[:, None], jnp.arange(cols)[None, :])
    return jnp.sum(jnp.where(tap[:, :, None] == jnp.arange(taps.shape[0]), taps, 0.0), -1)


def left(m):
    high, low = halves(m)
    return jnp.block([[high, high], [low, jnp.zeros_like(low)]])


def right(m):
    high, low = halves(m)
    return jnp.block([[high, low], [high, jnp.zeros_like(low)]])


def twice(m):
    none = jnp.zeros_like(m)
    return jnp.block([[m, none], [none, m]])


def operators(kernels):
    k = kernels / jnp.sum(kernels, axis=1, keepdims=True)
    along_y = band(k[1], PLANE, PLANE, lambda a, b: a - b + 15)
    along_x = band(k[2], PLANE, PLANE, lambda a, b: a - b + 15)
    blur_z = band(k[0], 2 * BATCH, 3 * BATCH, lambda row, col: 31 - (col - row))
    return_z = band(k[0], BATCH, 2 * BATCH, lambda row, col: col - row - 1)
    return (
        left(along_y), right(along_x.T), left(along_y.T), right(along_x),
        left(blur_z), twice(left(return_z)),
    )


def cost(us):
    return pl.CostEstimate(flops=int(us * 1.15e9), bytes_accessed=0, transcendentals=0)


PARAMS = pltpu.CompilerParams(vmem_limit_bytes=VMEM)
ANYWHERE = pl.BlockSpec(memory_space=pl.ANY)
WHOLE = pl.BlockSpec(memory_space=pltpu.VMEM)
SCALARS = pl.BlockSpec(memory_space=pltpu.SMEM)
SEGMENT = jax.ShapeDtypeStruct((PLANE, BATCH, PLANE), F32)


def two_planes(first, second, along_y, along_x):
    h0, l0 = split(first)
    h1, l1 = split(second)
    planes = jnp.concatenate(
        [jnp.concatenate([h0, h1], 1), jnp.concatenate([l0, l1], 1)], 0
    )
    out = jnp.dot(along_y, planes, preferred_element_type=F32)
    high, low = split(out[:PLANE] + out[PLANE:])
    rows = jnp.concatenate(
        [
            jnp.concatenate([high[:, :PLANE], low[:, :PLANE]], 1),
            jnp.concatenate([high[:, PLANE:], low[:, PLANE:]], 1),
        ],
        0,
    )
    out = jnp.dot(rows, along_x, preferred_element_type=F32)
    out = out[:, :PLANE] + out[:, PLANE:]
    return out[:PLANE], out[PLANE:]


def own_body(in_hbm, y_ref, x_ref, *refs):
    outs, (held, out, sem, out_sem) = refs[-7:-4], refs[-4:]
    reads = []
    for i in range(6):
        rows = pl.ds(16 * i, 16)
        reads.append(pltpu.make_async_copy(in_hbm.at[rows], held.at[rows], sem.at[i]))
        reads[-1].start()
    along_y, along_x = y_ref[...], x_ref[...]
    writes = []
    for batch in range(3):
        for i in range(BATCH // 2):
            if i % 8 == 0:
                reads[2 * batch + i // 8].wait()
            row = BATCH * batch + 2 * i
            out[batch, :, 2 * i, :], out[batch, :, 2 * i + 1, :] = two_planes(
                held[row], held[row + 1], along_y, along_x
            )
        writes.append(pltpu.make_async_copy(out.at[batch], outs[batch], out_sem.at[batch]))
        writes[-1].start()
    for copy in writes:
        copy.wait()


def lateral_own(volume, along_y, along_x, after):
    return pl.pallas_call(
        own_body,
        in_specs=[ANYWHERE] + [WHOLE] * 2 + [ANYWHERE] * len(after),
        out_specs=[ANYWHERE] * 3,
        out_shape=[SEGMENT] * 3,
        scratch_shapes=[
            pltpu.VMEM((BLOCK, PLANE, PLANE), F32),
            pltpu.VMEM((3, PLANE, BATCH, PLANE), F32),
            pltpu.SemaphoreType.DMA((6,)),
            pltpu.SemaphoreType.DMA((3,)),
        ],
        name="blur_own",
        cost_estimate=cost(0.5),
        compiler_params=PARAMS,
    )(volume, along_y, along_x, *after)


def chunks_of(refs):
    pair, second, own = refs
    return pair.at[0], pair.at[1], second, own


def pieces_body(sc_ref, *refs):
    y_ref, x_ref, out_ref, held, sem = refs[3:]
    copies = []
    for which, piece in enumerate(chunks_of(refs[:3])):
        spot = pl.ds(CHUNK * sc_ref[CHUNKS + which], CHUNK)
        copies.append(pltpu.make_async_copy(piece, held.at[spot], sem.at[which]))
        copies[-1].start()
    for copy in copies:
        copy.wait()
    along_y, along_x = y_ref[...], x_ref[...]
    for i in range(0, BATCH, 2):
        out_ref[:, i, :], out_ref[:, i + 1, :] = two_planes(held[i], held[i + 1], along_y, along_x)


def lateral_pieces(scalars, pieces, along_y, along_x):
    return pl.pallas_call(
        pieces_body,
        in_specs=[SCALARS] + [ANYWHERE] * 3 + [WHOLE] * 2,
        out_specs=WHOLE,
        out_shape=SEGMENT,
        scratch_shapes=[pltpu.VMEM((BATCH, PLANE, PLANE), F32), pltpu.SemaphoreType.DMA((4,))],
        name="blur_pieces",
        cost_estimate=cost(0.5),
        compiler_params=PARAMS,
    )(scalars, *pieces, along_y, along_x)


def send_out(held, which, outs, sem):
    first, second, own = outs
    target = first.at[which] if which in (FIRST, OTHER) else second if which == SECOND else own
    copy = pltpu.make_async_copy(held, target, sem.at[which])
    copy.start()
    return [copy]


def messages(rows):
    one = jax.ShapeDtypeStruct((rows, PLANE, PLANE), F32)
    return [jax.ShapeDtypeStruct((2, rows, PLANE, PLANE), F32), one, one]


def correct_body(batch, data_rows, waits, sc_ref, *refs):
    count = len(data_rows)
    parts, datas = refs[:3], refs[3 : 3 + count]
    w_hbm, blur_ref, back_ref, y_ref, x_ref = refs[3 + count : 8 + count]
    outs = refs[8 + count + waits : 11 + count + waits]
    t, d, w, returned, made, sem, out_sem = refs[11 + count + waits :]
    start = sc_ref[2]
    quarter = PLANE // QUARTERS
    reads = []
    for q in range(QUARTERS):
        side = pl.ds(quarter * q, quarter)
        now = [pltpu.make_async_copy(parts[i].at[side], t.at[i, side], sem.at[q, i]) for i in range(3)]
        for i, (row, rows, at) in enumerate(data_rows):
            now.append(
                pltpu.make_async_copy(
                    datas[i].at[pl.ds(row, rows), side], d.at[pl.ds(at, rows), side], sem.at[q, 3 + i]
                )
            )
        for copy in now:
            copy.start()
        reads.append(now)
    weight_copy = pltpu.make_async_copy(
        w_hbm.at[pl.ds(BATCH * batch, BATCH)], w, sem.at[QUARTERS, 0]
    )
    weight_copy.start()

    def quotient_of(y):
        high, low = zip(
            *[split(jnp.concatenate([t[i, y], t[i, y + 1]], 1)) for i in range(3)]
        )
        out = jnp.dot(blur_ref[...], jnp.concatenate(high + low, 0), preferred_element_type=F32)
        blurred = out[: 2 * BATCH] + out[2 * BATCH :] + BACKGROUND
        here = pl.ds(start, 2 * BATCH)
        data = jnp.concatenate([d[here, y, :], d[here, y + 1, :]], 1)
        return split(data / blurred)

    def rows_of(y):
        quotients = quotient_of(y) + quotient_of(y + 2)
        out = jnp.dot(
            back_ref[...], jnp.concatenate(quotients, 0), preferred_element_type=F32
        )
        for k in range(2):
            value = out[2 * BATCH * k :][:BATCH] + out[2 * BATCH * k + BATCH :][:BATCH]
            returned[:, y + 2 * k, :] = value[:, :PLANE]
            returned[:, y + 2 * k + 1, :] = value[:, PLANE:]

    for q in range(QUARTERS):
        for copy in reads[q]:
            copy.wait()

        @pl.loop(0, quarter // 32)
        def _(i):
            first = pl.multiple_of(quarter * q + 32 * i, 32)
            for y in range(0, 32, 4):
                rows_of(first + y)

    weight_copy.wait()
    along_y, along_x = y_ref[...], x_ref[...]
    writes = []
    for which in range(4):
        first = CHUNK * sc_ref[CHUNKS + which]
        for i in range(0, CHUNK, 2):
            pair = two_planes(returned[first + i], returned[first + i + 1], along_y, along_x)
            for k in range(2):
                value = pair[k] * w[first + i + k]
                inside = BATCH * batch + first + i + k >= sc_ref[1]
                made[which, i + k] = jnp.where(inside, value, 0.0)
        writes += send_out(made.at[which], which, outs, out_sem)
    for copy in writes:
        copy.wait()


def correct(scalars, batch, segments, data, weights, operator, after=()):
    low, own, high = data
    chosen = (
        ((low, 0, 32, 0), (own, 0, 48, 32)),
        ((own, 0, 80, 0),),
        ((own, 32, 64, 0), (high, 0, 16, 64)),
    )[batch]
    return pl.pallas_call(
        functools.partial(correct_body, batch, [rows[1:] for rows in chosen], len(after)),
        in_specs=[SCALARS] + [ANYWHERE] * (4 + len(chosen)) + [WHOLE] * 4 + [ANYWHERE] * len(after),
        out_specs=[ANYWHERE] * 3,
        out_shape=messages(CHUNK),
        scratch_shapes=[
            pltpu.VMEM((3, PLANE, BATCH, PLANE), F32),
            pltpu.VMEM((80, PLANE, PLANE), F32),
            pltpu.VMEM((BATCH, PLANE, PLANE), F32),
            pltpu.VMEM((BATCH, PLANE, PLANE), F32),
            pltpu.VMEM((4, CHUNK, PLANE, PLANE), F32),
            pltpu.SemaphoreType.DMA((QUARTERS + 1, 5)),
            pltpu.SemaphoreType.DMA((4,)),
        ],
        name="correct_batch",
        cost_estimate=cost(0.5),
        compiler_params=PARAMS,
    )(
        scalars, *segments, *[rows[0] for rows in chosen], weights,
        operator[4], operator[5], operator[2], operator[3], *after,
    )


def pick_body(chosen, waits, sc_ref, volume, *refs):
    outs, (held, sem, out_sem) = refs[waits:-3], refs[-3:]
    targets = {FIRST: outs[0].at[0], OTHER: outs[0].at[1]} if FIRST in chosen else dict(zip(chosen, outs))
    reads, writes = [], []
    for i, which in enumerate(chosen):
        chunk = sc_ref[CHUNKS + which]
        for batch in range(3):
            reads.append(
                pltpu.make_async_copy(
                    volume.at[pl.ds(BATCH * batch + CHUNK * chunk, CHUNK)],
                    held.at[i, pl.ds(CHUNK * batch, CHUNK)],
                    sem.at[3 * i + batch],
                )
            )
            reads[-1].start()
    for i, which in enumerate(chosen):
        for copy in reads[3 * i : 3 * i + 3]:
            copy.wait()
        writes.append(pltpu.make_async_copy(held.at[i], targets[which], out_sem.at[i]))
        writes[-1].start()
    for copy in writes:
        copy.wait()


def pick(scalars, volume, chosen, after=()):
    rows = 3 * CHUNK
    pair, one, _ = messages(rows)
    outs = [pair] if FIRST in chosen else [one] * len(chosen)
    return pl.pallas_call(
        functools.partial(pick_body, chosen, len(after)),
        in_specs=[SCALARS, ANYWHERE] + [ANYWHERE] * len(after),
        out_specs=[ANYWHERE] * len(outs),
        out_shape=outs,
        scratch_shapes=[
            pltpu.VMEM((len(chosen), rows, PLANE, PLANE), F32),
            pltpu.SemaphoreType.DMA((3 * len(chosen),)),
            pltpu.SemaphoreType.DMA((len(chosen),)),
        ],
        name="pick_chunks",
        cost_estimate=cost(1.4 * len(chosen)),
        compiler_params=PARAMS,
    )(scalars, volume, *after)


def assemble_body(batch, sc_ref, *refs):
    out, held, sem, out_sem = refs[-4:]
    reads, writes = [], []
    for which, piece in enumerate(chunks_of(refs[:3])):
        row = BATCH * batch + CHUNK * sc_ref[CHUNKS + which]
        reads.append(pltpu.make_async_copy(piece, held.at[which], sem.at[which]))
        reads[-1].start()
        writes.append(
            pltpu.make_async_copy(held.at[which], out.at[pl.ds(row, CHUNK)], out_sem.at[which])
        )
    for read, write in zip(reads, writes):
        read.wait()
        write.start()
    for copy in writes:
        copy.wait()


def assemble(scalars, batch, pieces, whole):
    earlier = [] if whole is None else [whole]
    return pl.pallas_call(
        functools.partial(assemble_body, batch),
        in_specs=[SCALARS] + [ANYWHERE] * (3 + len(earlier)),
        out_specs=ANYWHERE,
        out_shape=jax.ShapeDtypeStruct((BLOCK, PLANE, PLANE), F32),
        scratch_shapes=[
            pltpu.VMEM((4, CHUNK, PLANE, PLANE), F32),
            pltpu.SemaphoreType.DMA((4,)),
            pltpu.SemaphoreType.DMA((4,)),
        ],
        input_output_aliases={4: 0} if earlier else {},
        name="assemble",
        cost_estimate=cost(0.5),
        compiler_params=PARAMS,
    )(scalars, *pieces, *earlier)


def elementwise_call(body, name, us, outs, args, after=()):
    def kernel(*refs):
        body(*refs[: len(args)], *refs[len(args) + len(after) :])

    return pl.pallas_call(
        kernel,
        in_specs=[WHOLE] * len(args) + [ANYWHERE] * len(after),
        out_specs=[WHOLE] * len(outs),
        out_shape=outs,
        name=name,
        cost_estimate=cost(0.5),
        compiler_params=PARAMS,
    )(*args, *after)


def add_body(second, arrived, out):
    out[...] = second[...] + arrived[1]


def update_body(estimate, own, arrived, last, weight, out):
    out[...] = estimate[...] * (own[...] + arrived[0] + last[...]) / weight[...]


def total_body(own, arrived, last, out):
    out[...] = own[...] + arrived[0] + last[...]


def join_body(own, second, out):
    out[0] = own[...]
    out[1] = second[...]


def like(array, *lead):
    return jax.ShapeDtypeStruct((*lead, *array.shape), F32)


def exchange(value, turn):
    count = lax.axis_size("space")
    pairs = []
    for view in range(4):
        for place in range(count):
            partner = view ^ (1, 3)[(place + turn) % 2]
            pairs.append((view * count + place, partner * count + place))
    return lax.ppermute(value, ("view", "space"), pairs)


def to_space(value, steps):
    count = lax.axis_size("space")
    pairs = [(i, i + steps) for i in range(count) if 0 <= i + steps < count]
    return lax.ppermute(value, "space", pairs)


def on_device(estimate, view_data, blend_weights, kernels, shifts):
    view, place = lax.axis_index("view"), lax.axis_index("space")
    shift = shifts[0]
    near = jnp.where(place % 2 == 0, 1, 3)
    scalars = jnp.stack(
        [
            view, jnp.where(place == 0, shift, 0), 16 - shift,
            view ^ near, view ^ 2, view ^ near ^ 2, view,
        ]
    ).astype(jnp.int32)
    data, weights = view_data[0], blend_weights[0]
    operator = operators(kernels[0])

    (first_weights,) = pick(scalars, weights, (FIRST, OTHER))
    weight_first = exchange(first_weights, 0)
    data, first_weights = lax.optimization_barrier((data, first_weights))
    sides = data[BLOCK - 32 :], data[:16]
    data = to_space(sides[0], 1), data, to_space(sides[1], -1)
    segments = lateral_own(
        estimate, operator[0], operator[1], [first_weights, *sides]
    )
    line = [to_space(segments[2], 1), *segments, to_space(segments[0], -1)]
    own = whole = weight_sum = None
    for iteration in range(ITERS):
        order = (1, 0, 2) if iteration == 0 else (1, 2, 0)
        message, first, added, last, back, gathered = {}, {}, {}, {}, {}, {}

        def compute(batch, after=()):
            message[batch] = correct(
                scalars, batch, line[batch : batch + 3], data, weights, operator, after
            )
            first[batch] = exchange(message[batch][0], 0)

        def add(batch, after=()):
            second = message[batch][1]
            (added[batch],) = elementwise_call(
                add_body, "add", 2, [like(second)], (second, first[batch]), after
            )
            last[batch] = exchange(added[batch], 1)

        def update(batch, after=()):
            (own[batch],) = elementwise_call(
                update_body, "update", 2, [like(own[batch])],
                (own[batch], message[batch][2], first[batch], last[batch], weight_sum[batch]),
                after,
            )
            back[batch] = exchange(own[batch], 1)

        def join(batch, after=()):
            (pair,) = elementwise_call(
                join_body, "join", 2, [like(own[batch], 2)], (own[batch], back[batch]), after
            )
            gathered[batch] = exchange(pair, 0), back[batch], own[batch]

        x, y, z = order
        early = iteration == 0
        if early:
            compute(x, [data[0], data[2]])
            second_weights, own_weights = pick(scalars, weights, (SECOND, OWN), [*sides, message[x][1]])
            (estimates,) = pick(scalars, estimate, (OWN,), [*sides, message[x][1]])
            own = [estimates[CHUNK * b : CHUNK * b + CHUNK] for b in range(3)]
            (weight_added,) = elementwise_call(
                add_body, "add", 3, [like(second_weights)], (second_weights, weight_first), message[x][1:2]
            )
            weight_last = exchange(weight_added, 1)
            compute(y, [weight_added, line[0], line[4]])
            add(x, message[y][1:2])
            compute(z, [added[x]])
            (total,) = elementwise_call(
                total_body, "weight_total", 4, [like(own_weights)],
                (own_weights, weight_first, weight_last), message[z][1:2]
            )
            weight_sum = [total[CHUNK * b : CHUNK * b + CHUNK] for b in range(3)]
            add(y, [total])
        else:
            compute(x)
            compute(y, message[x][1:2])
            add(x, message[y][1:2])
            compute(z, [added[x]])
            add(y, message[z][1:2])
        update(x, [added[y]])
        add(z, [own[x]])
        update(y, [added[z]])
        join(x, [own[y]])
        update(z, [gathered[x][1]])
        join(y, [own[z]])
        join(z)
        if iteration == ITERS - 1:
            for batch in order:
                whole = assemble(scalars, batch, gathered[batch], whole)
            return whole
        segments = [None] * 3
        for batch in order:
            segments[batch] = lateral_pieces(scalars, gathered[batch], operator[0], operator[1])
        line = [to_space(segments[2], 1), *segments, to_space(segments[0], -1)]


def solution(mesh):
    return jax.shard_map(
        on_device,
        mesh=mesh,
        in_specs=(
            P("space", None, None),
            P("view", "space", None, None),
            P("view", "space", None, None),
            P("view", None, None),
            P("view"),
        ),
        out_specs=P("space", None, None),
        check_vma=False,
    )
```

```python
import functools

import jax
import jax.numpy as jnp
from jax import lax
from jax.experimental import pallas as pl
from jax.experimental.pallas import tpu as pltpu
from jax.sharding import PartitionSpec as P

F32, BF16 = jnp.float32, jnp.bfloat16
ITERS = 2
BACKGROUND = 0.1
BLOCK = 96
BATCH = 32
QUARTERS = 4
CHUNK = 8
PLANE = 128
VMEM = 50 << 20
FIRST, OTHER, SECOND, OWN = range(4)
CHUNKS = 3


def halves(m):
    high = lax.reduce_precision(m, 8, 7)
    return high.astype(BF16), (m - high).astype(BF16)


def split(value):
    high = value.astype(BF16)
    return high, (value - high.astype(F32)).astype(BF16)


def band(taps, rows, cols, index):
    tap = index(jnp.arange(rows)[:, None], jnp.arange(cols)[None, :])
    return jnp.sum(jnp.where(tap[:, :, None] == jnp.arange(taps.shape[0]), taps, 0.0), -1)


def left(m):
    high, low = halves(m)
    return jnp.block([[high, high], [low, jnp.zeros_like(low)]])


def right(m):
    high, low = halves(m)
    return jnp.block([[high, low], [high, jnp.zeros_like(low)]])


def twice(m):
    none = jnp.zeros_like(m)
    return jnp.block([[m, none], [none, m]])


def operators(kernels):
    k = kernels / jnp.sum(kernels, axis=1, keepdims=True)
    along_y = band(k[1], PLANE, PLANE, lambda a, b: a - b + 15)
    along_x = band(k[2], PLANE, PLANE, lambda a, b: a - b + 15)
    blur_z = band(k[0], 2 * BATCH, 3 * BATCH, lambda row, col: 31 - (col - row))
    return_z = band(k[0], BATCH, 2 * BATCH, lambda row, col: col - row - 1)
    return (
        left(along_y), right(along_x.T), left(along_y.T), right(along_x),
        left(blur_z), twice(left(return_z)),
    )


def cost(us):
    return pl.CostEstimate(flops=int(us * 1.15e9), bytes_accessed=0, transcendentals=0)


PARAMS = pltpu.CompilerParams(vmem_limit_bytes=VMEM)
ANYWHERE = pl.BlockSpec(memory_space=pl.ANY)
WHOLE = pl.BlockSpec(memory_space=pltpu.VMEM)
SCALARS = pl.BlockSpec(memory_space=pltpu.SMEM)
SEGMENT = jax.ShapeDtypeStruct((PLANE, BATCH, PLANE), F32)


def two_planes(first, second, along_y, along_x):
    h0, l0 = split(first)
    h1, l1 = split(second)
    planes = jnp.concatenate(
        [jnp.concatenate([h0, h1], 1), jnp.concatenate([l0, l1], 1)], 0
    )
    out = jnp.dot(along_y, planes, preferred_element_type=F32)
    high, low = split(out[:PLANE] + out[PLANE:])
    rows = jnp.concatenate(
        [
            jnp.concatenate([high[:, :PLANE], low[:, :PLANE]], 1),
            jnp.concatenate([high[:, PLANE:], low[:, PLANE:]], 1),
        ],
        0,
    )
    out = jnp.dot(rows, along_x, preferred_element_type=F32)
    out = out[:, :PLANE] + out[:, PLANE:]
    return out[:PLANE], out[PLANE:]


def own_body(in_hbm, y_ref, x_ref, *refs):
    outs, (held, out, sem, out_sem) = refs[-7:-4], refs[-4:]
    reads = []
    for i in range(6):
        rows = pl.ds(16 * i, 16)
        reads.append(pltpu.make_async_copy(in_hbm.at[rows], held.at[rows], sem.at[i]))
        reads[-1].start()
    along_y, along_x = y_ref[...], x_ref[...]
    writes = []
    for batch in range(3):
        for i in range(BATCH // 2):
            if i % 8 == 0:
                reads[2 * batch + i // 8].wait()
            row = BATCH * batch + 2 * i
            out[batch, :, 2 * i, :], out[batch, :, 2 * i + 1, :] = two_planes(
                held[row], held[row + 1], along_y, along_x
            )
        writes.append(pltpu.make_async_copy(out.at[batch], outs[batch], out_sem.at[batch]))
        writes[-1].start()
    for copy in writes:
        copy.wait()


def lateral_own(volume, along_y, along_x, after):
    return pl.pallas_call(
        own_body,
        in_specs=[ANYWHERE] + [WHOLE] * 2 + [ANYWHERE] * len(after),
        out_specs=[ANYWHERE] * 3,
        out_shape=[SEGMENT] * 3,
        scratch_shapes=[
            pltpu.VMEM((BLOCK, PLANE, PLANE), F32),
            pltpu.VMEM((3, PLANE, BATCH, PLANE), F32),
            pltpu.SemaphoreType.DMA((6,)),
            pltpu.SemaphoreType.DMA((3,)),
        ],
        name="blur_own",
        cost_estimate=cost(0.5),
        compiler_params=PARAMS,
    )(volume, along_y, along_x, *after)


def chunks_of(refs):
    pair, second, own = refs
    return pair.at[0], pair.at[1], second, own


def pieces_body(sc_ref, *refs):
    y_ref, x_ref, out_ref, held, sem = refs[3:]
    copies = []
    for which, piece in enumerate(chunks_of(refs[:3])):
        spot = pl.ds(CHUNK * sc_ref[CHUNKS + which], CHUNK)
        copies.append(pltpu.make_async_copy(piece, held.at[spot], sem.at[which]))
        copies[-1].start()
    for copy in copies:
        copy.wait()
    along_y, along_x = y_ref[...], x_ref[...]
    for i in range(0, BATCH, 2):
        out_ref[:, i, :], out_ref[:, i + 1, :] = two_planes(held[i], held[i + 1], along_y, along_x)


def lateral_pieces(scalars, pieces, along_y, along_x):
    return pl.pallas_call(
        pieces_body,
        in_specs=[SCALARS] + [ANYWHERE] * 3 + [WHOLE] * 2,
        out_specs=WHOLE,
        out_shape=SEGMENT,
        scratch_shapes=[pltpu.VMEM((BATCH, PLANE, PLANE), F32), pltpu.SemaphoreType.DMA((4,))],
        name="blur_pieces",
        cost_estimate=cost(0.5),
        compiler_params=PARAMS,
    )(scalars, *pieces, along_y, along_x)


def send_out(held, which, outs, sem):
    first, second, own = outs
    target = first.at[which] if which in (FIRST, OTHER) else second if which == SECOND else own
    copy = pltpu.make_async_copy(held, target, sem.at[which])
    copy.start()
    return [copy]


def messages(rows):
    one = jax.ShapeDtypeStruct((rows, PLANE, PLANE), F32)
    return [jax.ShapeDtypeStruct((2, rows, PLANE, PLANE), F32), one, one]


def correct_body(batch, data_rows, waits, sc_ref, *refs):
    count = len(data_rows)
    parts, datas = refs[:3], refs[3 : 3 + count]
    w_hbm, blur_ref, back_ref, y_ref, x_ref = refs[3 + count : 8 + count]
    outs = refs[8 + count + waits : 11 + count + waits]
    t, d, w, returned, made, sem, out_sem = refs[11 + count + waits :]
    start = sc_ref[2]
    quarter = PLANE // QUARTERS
    reads = []
    for q in range(QUARTERS):
        side = pl.ds(quarter * q, quarter)
        now = [pltpu.make_async_copy(parts[i].at[side], t.at[i, side], sem.at[q, i]) for i in range(3)]
        for i, (row, rows, at) in enumerate(data_rows):
            now.append(
                pltpu.make_async_copy(
                    datas[i].at[pl.ds(row, rows), side], d.at[pl.ds(at, rows), side], sem.at[q, 3 + i]
                )
            )
        for copy in now:
            copy.start()
        reads.append(now)
    weight_copy = pltpu.make_async_copy(
        w_hbm.at[pl.ds(BATCH * batch, BATCH)], w, sem.at[QUARTERS, 0]
    )
    weight_copy.start()

    def quotient_of(y):
        high, low = zip(
            *[split(jnp.concatenate([t[i, y], t[i, y + 1]], 1)) for i in range(3)]
        )
        out = jnp.dot(blur_ref[...], jnp.concatenate(high + low, 0), preferred_element_type=F32)
        blurred = out[: 2 * BATCH] + out[2 * BATCH :] + BACKGROUND
        here = pl.ds(start, 2 * BATCH)
        data = jnp.concatenate([d[here, y, :], d[here, y + 1, :]], 1)
        return split(data / blurred)

    def rows_of(y):
        quotients = quotient_of(y) + quotient_of(y + 2)
        out = jnp.dot(
            back_ref[...], jnp.concatenate(quotients, 0), preferred_element_type=F32
        )
        for k in range(2):
            value = out[2 * BATCH * k :][:BATCH] + out[2 * BATCH * k + BATCH :][:BATCH]
            returned[:, y + 2 * k, :] = value[:, :PLANE]
            returned[:, y + 2 * k + 1, :] = value[:, PLANE:]

    for q in range(QUARTERS):
        for copy in reads[q]:
            copy.wait()

        @pl.loop(0, quarter // 32)
        def _(i):
            first = pl.multiple_of(quarter * q + 32 * i, 32)
            for y in range(0, 32, 4):
                rows_of(first + y)

    weight_copy.wait()
    along_y, along_x = y_ref[...], x_ref[...]
    writes = []
    for which in range(4):
        first = CHUNK * sc_ref[CHUNKS + which]
        for i in range(0, CHUNK, 2):
            pair = two_planes(returned[first + i], returned[first + i + 1], along_y, along_x)
            for k in range(2):
                value = pair[k] * w[first + i + k]
                inside = BATCH * batch + first + i + k >= sc_ref[1]
                made[which, i + k] = jnp.where(inside, value, 0.0)
        writes += send_out(made.at[which], which, outs, out_sem)
    for copy in writes:
        copy.wait()


def correct(scalars, batch, segments, data, weights, operator, after=()):
    low, own, high = data
    chosen = (
        ((low, 0, 32, 0), (own, 0, 48, 32)),
        ((own, 0, 80, 0),),
        ((own, 32, 64, 0), (high, 0, 16, 64)),
    )[batch]
    return pl.pallas_call(
        functools.partial(correct_body, batch, [rows[1:] for rows in chosen], len(after)),
        in_specs=[SCALARS] + [ANYWHERE] * (4 + len(chosen)) + [WHOLE] * 4 + [ANYWHERE] * len(after),
        out_specs=[ANYWHERE] * 3,
        out_shape=messages(CHUNK),
        scratch_shapes=[
            pltpu.VMEM((3, PLANE, BATCH, PLANE), F32),
            pltpu.VMEM((80, PLANE, PLANE), F32),
            pltpu.VMEM((BATCH, PLANE, PLANE), F32),
            pltpu.VMEM((BATCH, PLANE, PLANE), F32),
            pltpu.VMEM((4, CHUNK, PLANE, PLANE), F32),
            pltpu.SemaphoreType.DMA((QUARTERS + 1, 5)),
            pltpu.SemaphoreType.DMA((4,)),
        ],
        name="correct_batch",
        cost_estimate=cost(0.5),
        compiler_params=PARAMS,
    )(
        scalars, *segments, *[rows[0] for rows in chosen], weights,
        operator[4], operator[5], operator[2], operator[3], *after,
    )


def pick_body(chosen, waits, sc_ref, volume, *refs):
    outs, (held, sem, out_sem) = refs[waits:-3], refs[-3:]
    targets = {FIRST: outs[0].at[0], OTHER: outs[0].at[1]} if FIRST in chosen else dict(zip(chosen, outs))
    reads, writes = [], []
    for i, which in enumerate(chosen):
        chunk = sc_ref[CHUNKS + which]
        for batch in range(3):
            reads.append(
                pltpu.make_async_copy(
                    volume.at[pl.ds(BATCH * batch + CHUNK * chunk, CHUNK)],
                    held.at[i, pl.ds(CHUNK * batch, CHUNK)],
                    sem.at[3 * i + batch],
                )
            )
            reads[-1].start()
    for i, which in enumerate(chosen):
        for copy in reads[3 * i : 3 * i + 3]:
            copy.wait()
        writes.append(pltpu.make_async_copy(held.at[i], targets[which], out_sem.at[i]))
        writes[-1].start()
    for copy in writes:
        copy.wait()


def pick(scalars, volume, chosen, after=()):
    rows = 3 * CHUNK
    pair, one, _ = messages(rows)
    outs = [pair] if FIRST in chosen else [one] * len(chosen)
    return pl.pallas_call(
        functools.partial(pick_body, chosen, len(after)),
        in_specs=[SCALARS, ANYWHERE] + [ANYWHERE] * len(after),
        out_specs=[ANYWHERE] * len(outs),
        out_shape=outs,
        scratch_shapes=[
            pltpu.VMEM((len(chosen), rows, PLANE, PLANE), F32),
            pltpu.SemaphoreType.DMA((3 * len(chosen),)),
            pltpu.SemaphoreType.DMA((len(chosen),)),
        ],
        name="pick_chunks",
        cost_estimate=cost(1.4 * len(chosen)),
        compiler_params=PARAMS,
    )(scalars, volume, *after)


def assemble_body(batch, sc_ref, *refs):
    out, held, sem, out_sem = refs[-4:]
    reads, writes = [], []
    for which, piece in enumerate(chunks_of(refs[:3])):
        row = BATCH * batch + CHUNK * sc_ref[CHUNKS + which]
        reads.append(pltpu.make_async_copy(piece, held.at[which], sem.at[which]))
        reads[-1].start()
        writes.append(
            pltpu.make_async_copy(held.at[which], out.at[pl.ds(row, CHUNK)], out_sem.at[which])
        )
    for read, write in zip(reads, writes):
        read.wait()
        write.start()
    for copy in writes:
        copy.wait()


def assemble(scalars, batch, pieces, whole):
    earlier = [] if whole is None else [whole]
    return pl.pallas_call(
        functools.partial(assemble_body, batch),
        in_specs=[SCALARS] + [ANYWHERE] * (3 + len(earlier)),
        out_specs=ANYWHERE,
        out_shape=jax.ShapeDtypeStruct((BLOCK, PLANE, PLANE), F32),
        scratch_shapes=[
            pltpu.VMEM((4, CHUNK, PLANE, PLANE), F32),
            pltpu.SemaphoreType.DMA((4,)),
            pltpu.SemaphoreType.DMA((4,)),
        ],
        input_output_aliases={4: 0} if earlier else {},
        name="assemble",
        cost_estimate=cost(0.5),
        compiler_params=PARAMS,
    )(scalars, *pieces, *earlier)


def elementwise_call(body, name, us, outs, args, after=()):
    def kernel(*refs):
        body(*refs[: len(args)], *refs[len(args) + len(after) :])

    return pl.pallas_call(
        kernel,
        in_specs=[WHOLE] * len(args) + [ANYWHERE] * len(after),
        out_specs=[WHOLE] * len(outs),
        out_shape=outs,
        name=name,
        cost_estimate=cost(0.5),
        compiler_params=PARAMS,
    )(*args, *after)


def add_body(second, arrived, out):
    out[...] = second[...] + arrived[1]


def update_body(estimate, own, arrived, last, weight, out):
    out[...] = estimate[...] * (own[...] + arrived[0] + last[...]) / weight[...]


def total_body(own, arrived, last, out):
    out[...] = own[...] + arrived[0] + last[...]


def join_body(own, second, out):
    out[0] = own[...]
    out[1] = second[...]


def like(array, *lead):
    return jax.ShapeDtypeStruct((*lead, *array.shape), F32)


def exchange(value, turn):
    count = lax.axis_size("space")
    pairs = []
    for view in range(4):
        for place in range(count):
            partner = view ^ (1, 3)[(place + turn) % 2]
            pairs.append((view * count + place, partner * count + place))
    return lax.ppermute(value, ("view", "space"), pairs)


def to_space(value, steps):
    count = lax.axis_size("space")
    pairs = [(i, i + steps) for i in range(count) if 0 <= i + steps < count]
    return lax.ppermute(value, "space", pairs)


def on_device(estimate, view_data, blend_weights, kernels, shifts):
    view, place = lax.axis_index("view"), lax.axis_index("space")
    shift = shifts[0]
    near = jnp.where(place % 2 == 0, 1, 3)
    scalars = jnp.stack(
        [
            view, jnp.where(place == 0, shift, 0), 16 - shift,
            view ^ near, view ^ 2, view ^ near ^ 2, view,
        ]
    ).astype(jnp.int32)
    data, weights = view_data[0], blend_weights[0]
    operator = operators(kernels[0])

    (first_weights,) = pick(scalars, weights, (FIRST, OTHER))
    weight_first = exchange(first_weights, 0)
    data, first_weights = lax.optimization_barrier((data, first_weights))
    sides = data[BLOCK - 32 :], data[:16]
    data = to_space(sides[0], 1), data, to_space(sides[1], -1)
    second_weights, own_weights = pick(scalars, weights, (SECOND, OWN), sides)
    (estimates,) = pick(scalars, estimate, (OWN,), sides)
    own = [estimates[CHUNK * b : CHUNK * b + CHUNK] for b in range(3)]
    segments = lateral_own(
        estimate, operator[0], operator[1], [first_weights, *sides, estimates, own_weights]
    )
    line = [to_space(segments[2], 1), *segments, to_space(segments[0], -1)]
    whole = weight_sum = None
    for iteration in range(ITERS):
        order = (1, 0, 2) if iteration == 0 else (1, 2, 0)
        message, first, added, last, back, gathered = {}, {}, {}, {}, {}, {}

        def compute(batch, after=()):
            message[batch] = correct(
                scalars, batch, line[batch : batch + 3], data, weights, operator, after
            )
            first[batch] = exchange(message[batch][0], 0)

        def add(batch, after=()):
            second = message[batch][1]
            (added[batch],) = elementwise_call(
                add_body, "add", 2, [like(second)], (second, first[batch]), after
            )
            last[batch] = exchange(added[batch], 1)

        def update(batch, after=()):
            (own[batch],) = elementwise_call(
                update_body, "update", 2, [like(own[batch])],
                (own[batch], message[batch][2], first[batch], last[batch], weight_sum[batch]),
                after,
            )
            back[batch] = exchange(own[batch], 1)

        def join(batch, after=()):
            (pair,) = elementwise_call(
                join_body, "join", 2, [like(own[batch], 2)], (own[batch], back[batch]), after
            )
            gathered[batch] = exchange(pair, 0), back[batch], own[batch]

        x, y, z = order
        early = iteration == 0
        if early:
            compute(x, [data[0], data[2]])
            (weight_added,) = elementwise_call(
                add_body, "add", 3, [like(second_weights)], (second_weights, weight_first), message[x][1:2]
            )
            weight_last = exchange(weight_added, 1)
            compute(y, [weight_added, line[0], line[4]])
            add(x, message[y][1:2])
            compute(z, [added[x]])
            (total,) = elementwise_call(
                total_body, "weight_total", 4, [like(own_weights)],
                (own_weights, weight_first, weight_last), message[z][1:2]
            )
            weight_sum = [total[CHUNK * b : CHUNK * b + CHUNK] for b in range(3)]
            add(y, [total])
        else:
            compute(x)
            compute(y, message[x][1:2])
            compute(z, [message[y][1], first[x]])
            add(x, message[z][1:2])
            add(y, [added[x]])
        update(x, [added[y]])
        add(z, [own[x]])
        update(y, [added[z]])
        join(x, [own[y]])
        update(z, [gathered[x][1]])
        join(y, [own[z]])
        join(z)
        if iteration == ITERS - 1:
            for batch in order:
                whole = assemble(scalars, batch, gathered[batch], whole)
            return whole
        segments = [None] * 3
        for batch in order:
            segments[batch] = lateral_pieces(scalars, gathered[batch], operator[0], operator[1])
        line = [to_space(segments[2], 1), *segments, to_space(segments[0], -1)]


def solution(mesh):
    return jax.shard_map(
        on_device,
        mesh=mesh,
        in_specs=(
            P("space", None, None),
            P("view", "space", None, None),
            P("view", "space", None, None),
            P("view", None, None),
            P("view"),
        ),
        out_specs=P("space", None, None),
        check_vma=False,
    )
```
